128 devices in a mesh: dp: 4 (over y), tm: 4 (over z), height: 8 (over x, core).
Axes of the slice: x: 4, y: 4, z: 4, core: 2. Of those that a mesh axis runs over, the one named last changes fastest.
Arguments:
- latents: bfloat16 [4, 8, 32, 160, 128], P('dp', 'tm', 'height'), may hold values from -40 to 40
- cotangent: bfloat16 [4, 8, 64, 320, 128], P('dp', 'tm', 'height'), may hold values from -6 to 6
- group_norm_gain: float32 [128], replicated, may hold values from 0.5 to 1.5
- group_norm_bias: float32 [128], replicated, may hold values from -3 to 3
- kernel: bfloat16 [3, 3, 384, 128], replicated, may hold values from -0.109375 to 0.109375
- kernel_bias: float32 [128], replicated, may hold values from -3 to 3
Outputs:
- upsampled: bfloat16 [4, 8, 64, 320, 128], P('dp', 'tm', 'height')
- latent_gradient: bfloat16 [4, 8, 32, 160, 128], P('dp', 'tm', 'height')
- kernel_grad: float32 [3, 3, 384, 128], replicated
- bias_grad: float32 [128], replicated
- gain_grad: float32 [128], replicated
- shift_grad: float32 [128], replicated
The draws below stay inside these ranges and needn't reach their ends.
All inputs are finite; a program needn't handle non-finite values.
Results may differ from the reference program's by a relative error of at most 0.0051.
Values may be sent and summed in bfloat16 or wider, within the bound.
A program may use at most 128 MiB of HBM per device.

```python
import jax
import jax.numpy as jnp
from jax import lax

C = 128
GROUPS = 32
WIDTH = 160
CLIPS = 4
FRAMES = 8
ROWS = 32


def draw_latents(key, part):
    shape = (CLIPS, FRAMES, ROWS, WIDTH, C)
    key_noise, key_rough, key_offset = jax.random.split(key, 3)
    frame_pos = jnp.arange(FRAMES, dtype=jnp.float32) / max(FRAMES - 1, 1)
    row_pos = jnp.arange(ROWS, dtype=jnp.float32) / max(ROWS - 1, 1)
    rising = 3.0 ** (0.5 * (frame_pos[:, None] + row_pos[None, :]))
    rough = jnp.exp(jax.random.uniform(key_rough, (CLIPS, FRAMES, ROWS, WIDTH, 1), jnp.float32, -0.7, 0.7))
    noise = jax.random.normal(key_noise, shape, jnp.float32)
    offset = jax.random.normal(key_offset, (CLIPS, 1, 1, 1, C), jnp.float32) * 0.5
    value = noise * rough * rising[None, :, :, None, None] + offset
    return jnp.clip(value, -40.0, 40.0).astype(jnp.bfloat16)


def level_of(own_key, shape, cuts, low, top_value):
    def one(axis_at, blocks):
        draws = jax.random.uniform(jax.random.fold_in(jax.random.fold_in(own_key, 6), axis_at), (blocks,), jnp.float32, low / len(cuts), top_value / len(cuts))
        return jnp.repeat(jnp.exp(draws), shape[axis_at] // blocks).reshape((-1,) + (1,) * (len(shape) - axis_at - 1))

    gain = one(*cuts[0])
    for cut in cuts[1:]:
        gain = gain * one(*cut)
    return gain


def normal_values(own_key, shape, deviation, most, pieces=(), kind=jnp.bfloat16):
    level = level_of(own_key, shape, pieces, -0.22, 0.18) if pieces else 1.0
    entries = jax.random.normal(own_key, shape, jnp.float32) * deviation * level
    return jnp.minimum(jnp.maximum(entries, -most), most).astype(kind)


def setup_inputs(seed: int = 0) -> dict:
    streams_of = jax.random.split(jax.random.key(seed), 7)
    latents = draw_latents(jax.random.fold_in(streams_of[6], 71), 0)
    cotangent = normal_values(streams_of[1], (CLIPS, FRAMES, 2 * ROWS, 2 * WIDTH, C), 1.0, 6.0, ((0, 4), (1, 4), (2, 8)))
    group_norm_gain = jnp.clip(jax.random.uniform(streams_of[2], (C,), jnp.float32, 0.5, 1.5), 0.5, 1.5)
    group_norm_bias = normal_values(streams_of[3], (C,), 0.5, 3.0, (), jnp.float32)
    kernel = normal_values(streams_of[4], (3, 3, 3 * C, C), (27 * C) ** -0.5, 0.109375)
    kernel_bias = normal_values(streams_of[5], (C,), 0.5, 3.0, (), jnp.float32)
    return dict(latents=latents, cotangent=cotangent, group_norm_gain=group_norm_gain, group_norm_bias=group_norm_bias, kernel=kernel, kernel_bias=kernel_bias)


def conv(padded, kernel, out_t, out_r, out_w):
    total = jnp.zeros((out_t * out_r * out_w, kernel.shape[-1]), jnp.float32)
    for i in range(3):
        for j in range(3):
            slab = jnp.concatenate([padded[i:i + out_t, j:j + out_r, k:k + out_w] for k in range(3)], axis=-1)
            total = total + jnp.dot(slab.reshape(-1, slab.shape[-1]), kernel[i, j], preferred_element_type=jnp.float32)
    return total.reshape(out_t, out_r, out_w, kernel.shape[-1])

def kernel_terms(padded, grad_out):
    out_t, out_r, out_w, channel_total = grad_out.shape
    flat = grad_out.reshape(-1, channel_total)
    rows_all = []
    for i in range(3):
        row_list = []
        for j in range(3):
            slab = jnp.concatenate([padded[i:i + out_t, j:j + out_r, k:k + out_w] for k in range(3)], axis=-1)
            row_list.append(lax.dot_general(slab.reshape(-1, slab.shape[-1]), flat, (((0,), (0,)), ((), ())), preferred_element_type=jnp.float32))
        rows_all.append(jnp.stack(row_list))
    return jnp.stack(rows_all)

def flip_kernel(kernel):
    channel_total = kernel.shape[-1]
    split = kernel.reshape(3, 3, 3, channel_total, channel_total)[::-1, ::-1, ::-1]
    return jnp.swapaxes(split, 3, 4).reshape(3, 3, 3 * channel_total, channel_total)

def edge_pad(value):
    return jnp.pad(value, ((2, 0), (1, 1), (1, 1), (0, 0)), mode='edge')

def one_clip(latent, cot, group_norm_gain, group_norm_bias, kernel, kernel_bias):
    frame_total, row_total, width_total, channel_total = latent.shape
    group_size = channel_total // GROUPS
    grouped = latent.astype(jnp.float32).reshape(frame_total, row_total, width_total, GROUPS, group_size)
    group_mean = lax.optimization_barrier(jnp.mean(grouped, axis=(0, 1, 2, 4)))
    centred_input = grouped - group_mean[:, None]
    var = lax.optimization_barrier(jnp.mean(centred_input * centred_input, axis=(0, 1, 2, 4)))
    inverse_deviation = lax.rsqrt(var + 1e-06)
    normalized_times_gradient = centred_input * inverse_deviation[:, None]
    normalized_input = normalized_times_gradient.reshape(frame_total, row_total, width_total, channel_total)
    preactivation = normalized_input * group_norm_gain + group_norm_bias
    sig = jax.nn.sigmoid(preactivation)
    act = (preactivation * sig).astype(jnp.bfloat16)
    padded = edge_pad(act)
    conv_out = (conv(padded, kernel, frame_total, row_total, width_total) + kernel_bias).astype(jnp.bfloat16)
    upsampled = jnp.broadcast_to(conv_out[:, :, None, :, None, :], (frame_total, row_total, 2, width_total, 2, channel_total)).reshape(frame_total, 2 * row_total, 2 * width_total, channel_total)
    dconv32 = lax.optimization_barrier(jnp.sum(cot.astype(jnp.float32).reshape(frame_total, row_total, 2, width_total, 2, channel_total), axis=(2, 4)))
    bias_part = lax.optimization_barrier(jnp.sum(dconv32, axis=(0, 1, 2)))
    dconv = dconv32.astype(jnp.bfloat16)
    kernel_part = kernel_terms(padded, dconv)
    wide = jnp.pad(dconv, ((2, 2), (2, 2), (2, 2), (0, 0)))
    dpadded = conv(wide, flip_kernel(kernel), frame_total + 2, row_total + 2, width_total + 2)
    primal, pull = jax.vjp(edge_pad, jnp.zeros((frame_total, row_total, width_total, channel_total), jnp.float32))
    dact = pull(dpadded)[0]
    preact_gradient = dact * sig * (1.0 + preactivation * (1.0 - sig))
    gain_partial = lax.optimization_barrier(jnp.sum(preact_gradient * normalized_input, axis=(0, 1, 2)))
    shift_part = lax.optimization_barrier(jnp.sum(preact_gradient, axis=(0, 1, 2)))
    normalized_gradient = (preact_gradient * group_norm_gain).reshape(frame_total, row_total, width_total, GROUPS, group_size)
    first_mean = lax.optimization_barrier(jnp.mean(normalized_gradient, axis=(0, 1, 2, 4)))
    second_mean = lax.optimization_barrier(jnp.mean(normalized_gradient * normalized_times_gradient, axis=(0, 1, 2, 4)))
    latent_gradient = (inverse_deviation[:, None] * (normalized_gradient - first_mean[:, None] - normalized_times_gradient * second_mean[:, None])).reshape(frame_total, row_total, width_total, channel_total).astype(jnp.bfloat16)
    return (upsampled, latent_gradient, kernel_part, bias_part, gain_partial, shift_part)

def reference(latents, cotangent, group_norm_gain, group_norm_bias, kernel, kernel_bias):

    def step(pair):
        return one_clip(pair[0], pair[1], group_norm_gain, group_norm_bias, kernel, kernel_bias)
    upsampled, latent_gradient, kernel_parts, bias_parts, gain_parts, shift_parts = lax.map(step, (latents, cotangent))
    return (upsampled, latent_gradient, lax.optimization_barrier(jnp.sum(kernel_parts, axis=0)), lax.optimization_barrier(jnp.sum(bias_parts, axis=0)), lax.optimization_barrier(jnp.sum(gain_parts, axis=0)), lax.optimization_barrier(jnp.sum(shift_parts, axis=0)))
```

```python
import functools

import jax
import jax.numpy as jnp
from jax import lax
from jax.experimental import pallas as pl
from jax.experimental.pallas import tpu as pltpu
from jax.sharding import PartitionSpec as P

MESH = pl.DeviceIdType.MESH
GROUPS = 32
F32 = jnp.float32
BF16 = jnp.bfloat16

ORDER = {2: ("x", "y", "z"), 1: ("y", "z", "x"), 0: ("z", "x", "y")}


def body(
    count,
    lat_hbm,
    cot_hbm,
    gain_ref,
    bias_ref,
    ker_hbm,
    kbias_ref,
    up_hbm,
    lg_hbm,
    kg_hbm,
    small_ref,
    lat,
    cot,
    ker,
    kt,
    dc,
    dslab,
    aslab,
    line,
    pool,
    xhat_s,
    dsilu_s,
    act_s,
    actt,
    acc,
    up,
    lg,
    kg,
    g,
    rc,
    s1,
    r1,
    e2,
    e3,
    fin,
    st1,
    st2,
    gr1,
    gr2,
    gr3,
    lsem,
    osem,
    lat_ss,
    lat_rs,
    dc_ss,
    dc_rs,
    sm_ss,
    sm_rs,
    ar_ss,
    ar_rs,
):
    y = lax.axis_index("dp")
    z = lax.axis_index("tm")
    h = lax.axis_index("height")
    x = lax.div(h, 2)
    core = lax.rem(h, 2)
    first, last = z == 0, z == 3
    has_prev, has_next = z > 0, z < 3
    top, bottom = h == 0, h == 7
    has_up, has_down = h > 0, h < 7

    def peer(axis, d):
        if axis == "x":
            return {"height": 2 * lax.rem(x + d, 4) + core}
        if axis == "y":
            return {"dp": lax.rem(y + d, 4)}
        if axis == "z":
            return {"tm": lax.rem(z + d, 4)}
        if axis == "h":
            return {"height": lax.rem(h + d, 8)}
        return {"height": 2 * x + 1 - core}

    place = {"x": x, "y": y, "z": z, "h": h}
    size = {"x": 4, "y": 4, "z": 4, "h": 8}

    def remote(src, dst, ss, rs, to):
        return pltpu.make_async_remote_copy(
            src_ref=src, dst_ref=dst, send_sem=ss, recv_sem=rs, device_id=to, device_id_type=MESH
        )

    barrier = pltpu.get_barrier_semaphore()
    greeted = [peer("h", d) for d in range(1, 8)]
    greeted += [peer("z", d) for d in range(1, 4)] + [peer("y", d) for d in range(1, 4)]
    for to in greeted:
        pl.semaphore_signal(barrier, inc=1, device_id=to, device_id_type=MESH)

    loads = [
        pltpu.make_async_copy(cot_hbm.at[0, 0], cot.at[0], lsem.at[0]),
        pltpu.make_async_copy(lat_hbm.at[0], lat.at[2:4, 1:5], lsem.at[1]),
        pltpu.make_async_copy(cot_hbm.at[0, 1], cot.at[1], lsem.at[2]),
        pltpu.make_async_copy(ker_hbm, ker, lsem.at[3]),
    ]
    for c in loads:
        c.start()

    row16 = lax.broadcasted_iota(jnp.int32, (16, 128), 0)

    def grad_line(slot, r, v):
        line[8:168, :] = v
        line[7:8, :] = jnp.zeros((1, 128), F32)
        line[168:169, :] = jnp.zeros((1, 128), F32)
        dslab[slot, r, :, 128:256] = v.astype(BF16)
        dslab[slot, r, 16:160, 0:128] = line[25:169, :].astype(BF16)
        dslab[slot, r, 0:16, 0:128] = (
            line[9:25, :] + jnp.where(row16 == 0, v[0:16], 0.0)
        ).astype(BF16)
        dslab[slot, r, 0:144, 256:384] = line[7:151, :].astype(BF16)
        dslab[slot, r, 144:160, 256:384] = (
            line[151:167, :] + jnp.where(row16 == 15, v[144:160], 0.0)
        ).astype(BF16)

    def pool_frame(t, total):
        def step(r, total):
            a = cot[t, 2 * r].astype(F32) + cot[t, 2 * r + 1].astype(F32)
            pool[...] = a
            v32 = pool[pl.ds(0, 160, stride=2), :] + pool[pl.ds(1, 160, stride=2), :]
            total = total + v32.reshape(20, 8, 128).sum(axis=0)
            v = v32.astype(BF16)
            dc[t, r + 1] = v
            grad_line(3 * t, r + 1, v.astype(F32))
            return total

        return lax.fori_loop(0, 4, step, total)

    loads[0].wait()
    bias_total = pool_frame(0, jnp.zeros((8, 128), F32))
    loads[2].wait()
    bias_total = pool_frame(1, bias_total)

    loads[1].wait()

    def stat_step(n, carry):
        s, q = carry
        v = lat[2 + n // 4, 1 + n % 4].astype(F32).reshape(20, 8, 128)
        return s + v.sum(axis=0), q + (v * v).sum(axis=0)

    zero8 = jnp.zeros((8, 128), F32)
    s_sum, q_sum = lax.fori_loop(0, 8, stat_step, (zero8, zero8))
    row8 = lax.broadcasted_iota(jnp.int32, (8, 128), 0)

    def rows_of(*vectors):
        out = zero8
        for n, v in enumerate(vectors):
            out = jnp.where(row8 == n, v.sum(axis=0, keepdims=True), out)
        return out

    st1[h] = rows_of(s_sum, q_sum)

    pl.semaphore_wait(barrier, 13)

    def exchange_start(buf, axis, base):
        me = place[axis]
        out = []
        for d in range(1, size[axis]):
            c = remote(
                buf.at[me], buf.at[me], sm_ss.at[base + d], sm_rs.at[base + d], peer(axis, d)
            )
            c.start()
            out.append(c)
        return out

    def exchange_wait(copies):
        for c in copies:
            c.wait_recv()

    def tile_sum(buf, axis):
        out = buf[0]
        for n in range(1, size[axis]):
            out = out + buf[n]
        return out

    def dc_z(t, part):
        rows = (slice(1, 2), slice(4, 5), slice(2, 4))[part]
        n = 3 * t + part
        return remote(
            dc.at[t, rows],
            dc.at[2 + t, rows],
            dc_ss.at[n],
            dc_rs.at[n],
            {"tm": jnp.maximum(z - 1, 0)},
        )

    def dc_row(f, down):
        n = 6 + 2 * f + down
        src, dst = (4, 0) if down else (1, 5)
        to = {"height": jnp.minimum(h + 1, 7) if down else jnp.maximum(h - 1, 0)}
        return remote(dc.at[f, src], dc.at[f, dst], dc_ss.at[n], dc_rs.at[n], to)

    def lat_z(part):
        rows = (slice(1, 2), slice(4, 5), slice(2, 4))[part]
        return remote(
            lat.at[2:4, rows],
            lat.at[0:2, rows],
            lat_ss.at[part],
            lat_rs.at[part],
            {"tm": jnp.minimum(z + 1, 3)},
        )

    def lat_row(base, down):
        n = 3 + base + down
        src, dst = (4, 0) if down else (1, 5)
        to = {"height": jnp.minimum(h + 1, 7) if down else jnp.maximum(h - 1, 0)}
        return remote(
            lat.at[base : base + 2, src],
            lat.at[base : base + 2, dst],
            lat_ss.at[n],
            lat_rs.at[n],
            to,
        )

    stat_h = exchange_start(st1, "h", 0)

    @pl.when(has_prev)
    def _():
        for t in range(2):
            for part in range(3):
                dc_z(t, part).start()

    @pl.when(has_up)
    def _():
        dc_row(0, 0).start()
        dc_row(1, 0).start()
        lat_row(2, 0).start()

    @pl.when(has_down)
    def _():
        dc_row(0, 1).start()
        dc_row(1, 1).start()
        lat_row(2, 1).start()

    @pl.when(has_next)
    def _():
        for part in range(3):
            lat_z(part).start()

    exchange_wait(stat_h)
    st2[z] = tile_sum(st1, "h")
    stat_z = exchange_start(st2, "z", 8)

    loads[3].wait()

    def flip(n, carry):
        i, j = n // 3, n % 3
        for k in range(3):
            kt[i, pl.ds(pl.multiple_of(j * 384 + k * 128, 128), 128), :] = ker[
                i, j, k * 128 : (k + 1) * 128, :
            ].T
        return carry

    lax.fori_loop(0, 9, flip, 0)

    @pl.when(top)
    def _():
        for f in range(4):
            dc[f, 0] = jnp.zeros((160, 128), BF16)

    @pl.when(bottom)
    def _():
        for f in range(4):
            dc[f, 5] = jnp.zeros((160, 128), BF16)

    @pl.when(has_up)
    def _():
        dc_row(0, 1).wait_recv()
        dc_row(1, 1).wait_recv()

    @pl.when(has_down)
    def _():
        dc_row(0, 0).wait_recv()
        dc_row(1, 0).wait_recv()

    def grad_row(slot, f, r):
        grad_line(slot, r, dc[f, r].astype(F32))

    def edge_rows(n, carry):
        grad_row(3 * (n // 2), n // 2, 5 * (n % 2))
        return carry

    lax.fori_loop(0, 4, edge_rows, 0)

    def special_rows(slot):
        @pl.when(top)
        def _():
            dslab[slot, 6] = dslab[slot, 2] + dslab[slot, 1]

        @pl.when(bottom)
        def _():
            dslab[slot, 7] = dslab[slot, 3] + dslab[slot, 4]

    special_rows(0)
    special_rows(3)

    @pl.when(first)
    def _():
        def add(r, carry):
            dslab[1, r] = dslab[0, r] + dslab[3, r]
            return carry

        lax.fori_loop(0, 6, add, 0)
        special_rows(1)

    row_t = jnp.where(top, 6, 2)
    row_b = jnp.where(bottom, 7, 3)

    def taken(slot, j):
        if j == 0:
            parts = [dslab[pl.ds(slot, 1), pl.ds(row_t, 1)][0], dslab[slot, 3:6]]
        elif j == 1:
            parts = [dslab[slot, 1:5]]
        else:
            parts = [dslab[slot, 0:3], dslab[pl.ds(slot, 1), pl.ds(row_b, 1)][0]]
        v = jnp.concatenate(parts, axis=0) if len(parts) > 1 else parts[0]
        return v.reshape(640, 384)

    slot_of = {
        (0, 2): 0,
        (0, 1): jnp.where(first, 1, 3),
        (0, 0): jnp.where(first, 2, 4),
        (1, 2): 3,
        (1, 1): 4,
        (1, 0): 5,
    }

    exchange_wait(stat_z)
    lane_a = lax.broadcasted_iota(jnp.int32, (128, 128), 0) >> 2
    lane_b = lax.broadcasted_iota(jnp.int32, (128, 128), 1) >> 2
    same = jnp.where(lane_a == lane_b, 1.0, 0.0)

    def by_group(v):
        return jnp.dot(v, same, precision=lax.Precision.HIGHEST, preferred_element_type=F32)

    sums = by_group(tile_sum(st2, "z")) / count
    mean = sums[0:1]
    rstd = lax.rsqrt(sums[1:2] - mean * mean + 1e-6)
    gain = gain_ref[...]
    shift = bias_ref[...]

    def act_row(f, r, own):
        v = (lat[f, r].astype(F32) - mean) * rstd
        pre = v * gain + shift
        sig = 1.0 / (1.0 + jnp.exp(-pre))
        a = pre * sig
        if own:
            n = (f - 2) * 4 + r - 1
            rows = pl.ds(pl.multiple_of(n * 160, 160), 160)
            xhat_s[rows, :] = v
            dsilu_s[rows, :] = sig * (1.0 + pre * (1.0 - sig))
            act_s[rows, :] = a
        line[8:168, :] = a
        line[7:8, :] = a[0:1]
        line[168:169, :] = a[159:160]
        aslab[f, r, :, 0:128] = line[7:167, :].astype(BF16)
        aslab[f, r, :, 128:256] = a.astype(BF16)
        aslab[f, r, :, 256:384] = line[9:169, :].astype(BF16)

    def own_rows(n, carry):
        act_row(2 + n // 4, 1 + n % 4, True)
        return carry

    lax.fori_loop(0, 8, own_rows, 0)

    def transposed(n, carry):
        rows = pl.ds(pl.multiple_of(n * 128, 128), 128)
        actt[:, rows] = act_s[rows, :].T.astype(BF16)
        return carry

    lax.fori_loop(0, 10, transposed, 0)

    def weight_grad(i):
        for j in range(3):
            right = jnp.concatenate([taken(slot_of[0, i], j), taken(slot_of[1, i], j)], axis=0)
            part = jnp.dot(actt[...], right, preferred_element_type=F32)
            g[i, :, :, j * 384 : (j + 1) * 384] = part.astype(BF16).reshape(8, 16, 384)

    copies = {}

    def copy_c(i):
        c = remote(
            g.at[i, pl.ds((1 - core) * 4, 4)],
            rc.at[i],
            ar_ss.at[i, 0],
            ar_rs.at[i, 0],
            peer("core", 0),
        )
        c.start()
        copies[i, 0] = [c]

    def reduce_1(i):
        for c in copies[i, 0]:
            c.wait_recv()
        s1[i] = (g[i, pl.ds(core * 4, 4)].astype(F32) + rc[i].astype(F32)).astype(BF16)
        axis = ORDER[i][0]
        me = place[axis]
        copies[i, 1] = []
        for d in range(1, 4):
            c = remote(
                s1.at[i, lax.rem(me + d, 4)],
                r1.at[i, me],
                ar_ss.at[i, d],
                ar_rs.at[i, d],
                peer(axis, d),
            )
            c.start()
            copies[i, 1].append(c)
        r1[i, me] = s1[i, me]

    def exchange(i, step, buf):
        axis = ORDER[i][step - 1]
        me = place[axis]
        copies[i, step] = []
        for d in range(1, 4):
            n = 3 * (step - 1) + d
            c = remote(buf.at[i, me], buf.at[i, me], ar_ss.at[i, n], ar_rs.at[i, n], peer(axis, d))
            c.start()
            copies[i, step].append(c)

    def total_of(buf, i):
        out = buf[i, 0].astype(F32)
        for n in range(1, 4):
            out = out + buf[i, n].astype(F32)
        return out.astype(BF16)

    def reduce_2(i):
        for c in copies[i, 1]:
            c.wait_recv()
        e2[i, place[ORDER[i][1]]] = total_of(r1, i)
        exchange(i, 2, e2)

    def reduce_3(i):
        for c in copies[i, 2]:
            c.wait_recv()
        e3[i, place[ORDER[i][2]]] = total_of(e2, i)
        exchange(i, 3, e3)

    def gather_1(i):
        for c in copies[i, 3]:
            c.wait_recv()
        axis = ORDER[i][0]
        me = core * 4 + place[axis]
        fin[i, me] = total_of(e3, i)
        copies[i, 4] = []
        for d in range(1, 4):
            n = 9 + d
            c = remote(fin.at[i, me], fin.at[i, me], ar_ss.at[i, n], ar_rs.at[i, n], peer(axis, d))
            c.start()
            copies[i, 4].append(c)

    def gather_c(i):
        for c in copies[i, 4]:
            c.wait_recv()
        half = pl.ds(core * 4, 4)
        c = remote(
            fin.at[i, half], fin.at[i, half], ar_ss.at[i, 13], ar_rs.at[i, 13], peer("core", 0)
        )
        c.start()
        copies[i, 5] = [c]

    outs = []

    def finish(i):
        for c in copies[i, 5]:
            c.wait_recv()
        for n in range(9):
            j, k = divmod(n, 3)
            kg[i, j, k * 128 : (k + 1) * 128, :] = (
                fin[i, :, :, n * 128 : (n + 1) * 128].reshape(128, 128).astype(F32)
            )
        c = pltpu.make_async_copy(kg.at[i], kg_hbm.at[i], osem.at[i])
        c.start()
        outs.append(c)

    weight_grad(2)
    copy_c(2)

    @pl.when(last)
    def _():
        for f in range(2, 4):
            for r in range(6):
                dc[f, r] = jnp.zeros((160, 128), BF16)

    def ahead(t):
        f = 2 + t

        @pl.when(has_next)
        def _():
            dc_z(t, 0).wait_recv()
            dc_z(t, 1).wait_recv()

            @pl.when(has_up)
            def _():
                dc_row(f, 0).start()

            @pl.when(has_down)
            def _():
                dc_row(f, 1).start()

            dc_z(t, 2).wait_recv()

        def inner(r, carry):
            grad_row(4 + t, f, r)
            return carry

        lax.fori_loop(1, 5, inner, 0)

        @pl.when(has_next)
        def _():
            @pl.when(has_up)
            def _():
                dc_row(f, 1).wait_recv()

            @pl.when(has_down)
            def _():
                dc_row(f, 0).wait_recv()

        def outer(n, carry):
            grad_row(4 + t, f, 5 * n)
            return carry

        lax.fori_loop(0, 2, outer, 0)
        special_rows(4 + t)

    ahead(0)

    @pl.when(first)
    def _():
        def add(r, carry):
            dslab[2, r] = dslab[1, r] + dslab[4, r]
            return carry

        lax.fori_loop(0, 6, add, 0)
        special_rows(2)

    reduce_1(2)
    weight_grad(1)
    copy_c(1)
    ahead(1)
    reduce_2(2)
    reduce_1(1)
    weight_grad(0)
    copy_c(0)

    def data_grad(p):
        rows = slice(p * 640, (p + 1) * 640)
        for i in (2, 1, 0):
            left = jnp.concatenate([taken(slot_of[p, i], j) for j in range(3)], axis=1)
            part = lax.dot_general(
                left, kt[i], (((1,), (0,)), ((), ())), preferred_element_type=F32
            )
            acc[rows, :] = part if i == 2 else acc[rows, :] + part

    data_grad(0)
    reduce_3(2)
    reduce_2(1)
    reduce_1(0)
    data_grad(1)

    def through(n, carry):
        a, b = carry
        rows = pl.ds(pl.multiple_of(n * 160, 160), 160)
        d = acc[rows, :] * dsilu_s[rows, :]
        acc[rows, :] = d
        b = b + (d * xhat_s[rows, :]).reshape(20, 8, 128).sum(axis=0)
        return a + d.reshape(20, 8, 128).sum(axis=0), b

    d_sum, dx_sum = lax.fori_loop(0, 8, through, (zero8, zero8))
    gr1[h] = rows_of(d_sum, dx_sum, bias_total)
    grad_h = exchange_start(gr1, "h", 12)
    gather_1(2)
    reduce_3(1)
    reduce_2(0)

    @pl.when(top)
    def _():
        for f in range(2, 4):
            lat[f, 0] = lat[f, 1]

    @pl.when(bottom)
    def _():
        for f in range(2, 4):
            lat[f, 5] = lat[f, 4]

    @pl.when(has_up)
    def _():
        lat_row(2, 1).wait_recv()

    @pl.when(has_down)
    def _():
        lat_row(2, 0).wait_recv()

    @pl.when(has_prev)
    def _():
        lat_z(0).wait_recv()
        lat_z(1).wait_recv()

        @pl.when(has_up)
        def _():
            lat_row(0, 0).start()

        @pl.when(has_down)
        def _():
            lat_row(0, 1).start()

        lat_z(2).wait_recv()

        @pl.when(top)
        def _():
            for f in range(2):
                lat[f, 0] = lat[f, 1]

        @pl.when(bottom)
        def _():
            for f in range(2):
                lat[f, 5] = lat[f, 4]

        @pl.when(has_up)
        def _():
            lat_row(0, 1).wait_recv()

        @pl.when(has_down)
        def _():
            lat_row(0, 0).wait_recv()

    @pl.when(first)
    def _():
        for f in range(2):
            for r in range(6):
                lat[f, r] = lat[2, r]

    exchange_wait(grad_h)
    gr2[z] = tile_sum(gr1, "h")
    grad_z = exchange_start(gr2, "z", 20)

    def edge_act(n, carry):
        act_row(2 + n // 2, 5 * (n % 2), False)
        return carry

    lax.fori_loop(0, 4, edge_act, 0)

    def past_act(n, carry):
        act_row(n // 6, n % 6, False)
        return carry

    lax.fori_loop(0, 12, past_act, 0)
    gather_c(2)
    gather_1(1)
    reduce_3(0)
    exchange_wait(grad_z)
    clip_sums = tile_sum(gr2, "z")
    gr3[y] = clip_sums
    grad_y = exchange_start(gr3, "y", 24)

    means = by_group(clip_sums * gain) / count
    mean_a, mean_b = means[0:1], means[1:2]

    def latent_grad(n, carry):
        rows = pl.ds(pl.multiple_of(n * 160, 160), 160)
        v = rstd * (acc[rows, :] * gain - mean_a - xhat_s[rows, :] * mean_b)
        lg[n // 4, n % 4] = v.astype(BF16)
        return carry

    lax.fori_loop(0, 8, latent_grad, 0)
    c = pltpu.make_async_copy(lg, lg_hbm.at[0], osem.at[3])
    c.start()
    outs.append(c)

    kbias = kbias_ref[...]

    def conv(t):
        rows = slice(t * 640, (t + 1) * 640)
        for i in range(3):
            left = jnp.concatenate(
                [aslab[t + i, j : j + 4].reshape(640, 384) for j in range(3)], axis=1
            )
            part = jnp.dot(left, ker[i].reshape(1152, 128), preferred_element_type=F32)
            act_s[rows, :] = part if i == 0 else act_s[rows, :] + part

        def expand(r, carry):
            v = act_s[pl.ds(pl.multiple_of((t * 4 + r) * 160, 160), 160), :] + kbias
            pool[pl.ds(0, 160, stride=2), :] = v
            pool[pl.ds(1, 160, stride=2), :] = v
            w = pool[...].astype(BF16)
            up[t, 2 * r] = w
            up[t, 2 * r + 1] = w
            return carry

        lax.fori_loop(0, 4, expand, 0)
        c = pltpu.make_async_copy(up.at[t], up_hbm.at[0, t], osem.at[4 + t])
        c.start()
        outs.append(c)

    conv(0)
    finish(2)
    gather_c(1)
    gather_1(0)
    conv(1)
    finish(1)
    gather_c(0)
    exchange_wait(grad_y)
    small_ref[...] = tile_sum(gr3, "y")
    finish(0)

    for group in (stat_h, stat_z, grad_h, grad_z, grad_y, *copies.values()):
        for c in group:
            c.wait_send()

    @pl.when(has_prev)
    def _():
        for t in range(2):
            for part in range(3):
                dc_z(t, part).wait_send()

    @pl.when(has_next)
    def _():
        for part in range(3):
            lat_z(part).wait_send()

    for down, there in ((0, has_up), (1, has_down)):

        @pl.when(there)
        def _(down=down):
            dc_row(0, down).wait_send()
            dc_row(1, down).wait_send()
            lat_row(2, down).wait_send()

            @pl.when(has_next)
            def _():
                dc_row(2, down).wait_send()
                dc_row(3, down).wait_send()

            @pl.when(has_prev)
            def _():
                lat_row(0, down).wait_send()

    for c in outs:
        c.wait()


def local(latents, cotangent, gain, bias, kernel, kernel_bias):
    count = 8 * 32 * 160 * (128 // GROUPS)
    hbm = pl.BlockSpec(memory_space=pl.ANY)
    vmem = pl.BlockSpec(memory_space=pltpu.VMEM)
    dma = pltpu.SemaphoreType.DMA
    up, lg, kg, small = pl.pallas_call(
        functools.partial(body, float(count)),
        out_shape=(
            jax.ShapeDtypeStruct((1, 2, 8, 320, 128), BF16),
            jax.ShapeDtypeStruct((1, 2, 4, 160, 128), BF16),
            jax.ShapeDtypeStruct((3, 3, 384, 128), F32),
            jax.ShapeDtypeStruct((8, 128), F32),
        ),
        in_specs=[hbm, hbm, vmem, vmem, hbm, vmem],
        out_specs=(hbm, hbm, hbm, vmem),
        scratch_shapes=[
            pltpu.VMEM((4, 6, 160, 128), BF16),
            pltpu.VMEM((2, 8, 320, 128), BF16),
            pltpu.VMEM((3, 3, 384, 128), BF16),
            pltpu.VMEM((3, 1152, 128), BF16),
            pltpu.VMEM((4, 6, 160, 128), BF16),
            pltpu.VMEM((6, 8, 160, 384), BF16),
            pltpu.VMEM((4, 6, 160, 384), BF16),
            pltpu.VMEM((176, 128), F32),
            pltpu.VMEM((320, 128), F32),
            pltpu.VMEM((1280, 128), F32),
            pltpu.VMEM((1280, 128), F32),
            pltpu.VMEM((1280, 128), F32),
            pltpu.VMEM((128, 1280), BF16),
            pltpu.VMEM((1280, 128), F32),
            pltpu.VMEM((2, 8, 320, 128), BF16),
            pltpu.VMEM((2, 4, 160, 128), BF16),
            pltpu.VMEM((3, 3, 384, 128), F32),
            pltpu.VMEM((3, 8, 16, 1152), BF16),
            pltpu.VMEM((3, 4, 16, 1152), BF16),
            pltpu.VMEM((3, 4, 16, 1152), BF16),
            pltpu.VMEM((3, 4, 16, 1152), BF16),
            pltpu.VMEM((3, 4, 16, 1152), BF16),
            pltpu.VMEM((3, 4, 16, 1152), BF16),
            pltpu.VMEM((3, 8, 16, 1152), BF16),
            pltpu.VMEM((8, 8, 128), F32),
            pltpu.VMEM((4, 8, 128), F32),
            pltpu.VMEM((8, 8, 128), F32),
            pltpu.VMEM((4, 8, 128), F32),
            pltpu.VMEM((4, 8, 128), F32),
            dma((4,)),
            dma((6,)),
            dma((7,)),
            dma((7,)),
            dma((14,)),
            dma((14,)),
            dma((28,)),
            dma((28,)),
            dma((3, 14)),
            dma((3, 14)),
        ],
        compiler_params=pltpu.CompilerParams(
            collective_id=0, has_side_effects=True, vmem_limit_bytes=50 * 1024 * 1024
        ),
        cost_estimate=pl.CostEstimate(flops=3 * 2 * 1280 * 3456 * 128, bytes_accessed=6000000, transcendentals=500000),
    )(latents, cotangent, gain[None], bias[None], kernel, kernel_bias[None])
    return up, lg, kg, small[2], small[1], small[0]


def solution(mesh):
    split = P("dp", "tm", "height", None, None)
    return jax.shard_map(
        local,
        mesh=mesh,
        in_specs=(split, split, P(), P(), P(), P()),
        out_specs=(split, split, P(), P(), P(), P()),
        check_vma=False,
    )
```

```python
import functools

import jax
import jax.numpy as jnp
from jax import lax
from jax.experimental import pallas as pl
from jax.experimental.pallas import tpu as pltpu
from jax.sharding import PartitionSpec as P

MESH = pl.DeviceIdType.MESH
GROUPS = 32
F32 = jnp.float32
BF16 = jnp.bfloat16

ORDER = {2: ("x", "y", "z"), 1: ("y", "z", "x"), 0: ("z", "x", "y")}


def body(
    count,
    lat_hbm,
    cot_hbm,
    gain_hbm,
    bias_hbm,
    ker_hbm,
    kbias_hbm,
    up,
    lg,
    kg,
    small_ref,
    vec,
    lat,
    cot,
    ker,
    kt,
    dc,
    dslab,
    aslab,
    line,
    pool,
    xhat_s,
    act_s,
    actt,
    acc,
    cacc,
    g,
    rc,
    s1,
    r1,
    e2,
    e3,
    fin,
    st1,
    st2,
    gr1,
    gr2,
    gr3,
    lsem,
    lat_ss,
    lat_rs,
    dc_ss,
    dc_rs,
    sm_ss,
    sm_rs,
    ar_ss,
    ar_rs,
):
    y = lax.axis_index("dp")
    z = lax.axis_index("tm")
    h = lax.axis_index("height")
    x = lax.div(h, 2)
    core = lax.rem(h, 2)
    first, last = z == 0, z == 3
    has_prev, has_next = z > 0, z < 3
    top, bottom = h == 0, h == 7
    has_up, has_down = h > 0, h < 7

    def peer(axis, d):
        if axis == "x":
            return {"height": 2 * lax.rem(x + d, 4) + core}
        if axis == "y":
            return {"dp": lax.rem(y + d, 4)}
        if axis == "z":
            return {"tm": lax.rem(z + d, 4)}
        if axis == "h":
            return {"height": lax.rem(h + d, 8)}
        return {"height": 2 * x + 1 - core}

    place = {"x": x, "y": y, "z": z, "h": h}
    size = {"x": 4, "y": 4, "z": 4, "h": 8}

    def remote(src, dst, ss, rs, to):
        return pltpu.make_async_remote_copy(
            src_ref=src, dst_ref=dst, send_sem=ss, recv_sem=rs, device_id=to, device_id_type=MESH
        )

    barrier = pltpu.get_barrier_semaphore()
    greeted = [peer("h", d) for d in range(1, 8)]
    greeted += [peer("z", d) for d in range(1, 4)] + [peer("y", d) for d in range(1, 4)]
    for to in greeted:
        pl.semaphore_signal(barrier, inc=1, device_id=to, device_id_type=MESH)

    loads = [
        pltpu.make_async_copy(cot_hbm.at[0, 0], cot.at[0], lsem.at[0]),
        pltpu.make_async_copy(lat_hbm.at[0], lat.at[2:4, 1:5], lsem.at[1]),
        pltpu.make_async_copy(cot_hbm.at[0, 1], cot.at[1], lsem.at[2]),
        pltpu.make_async_copy(ker_hbm, ker, lsem.at[3]),
        pltpu.make_async_copy(gain_hbm, vec.at[0:1], lsem.at[4]),
        pltpu.make_async_copy(bias_hbm, vec.at[1:2], lsem.at[5]),
        pltpu.make_async_copy(kbias_hbm, vec.at[2:3], lsem.at[6]),
    ]
    for c in loads:
        c.start()

    row16 = lax.broadcasted_iota(jnp.int32, (16, 128), 0)

    def grad_line(slot, r, v):
        line[8:168, :] = v
        line[7:8, :] = jnp.zeros((1, 128), F32)
        line[168:169, :] = jnp.zeros((1, 128), F32)
        dslab[slot, r, :, 128:256] = v.astype(BF16)
        dslab[slot, r, 16:160, 0:128] = line[25:169, :].astype(BF16)
        dslab[slot, r, 0:16, 0:128] = (
            line[9:25, :] + jnp.where(row16 == 0, v[0:16], 0.0)
        ).astype(BF16)
        dslab[slot, r, 0:144, 256:384] = line[7:151, :].astype(BF16)
        dslab[slot, r, 144:160, 256:384] = (
            line[151:167, :] + jnp.where(row16 == 15, v[144:160], 0.0)
        ).astype(BF16)

    def pool_frame(t, total):
        def step(r, total):
            a = cot[t, 2 * r].astype(F32) + cot[t, 2 * r + 1].astype(F32)
            pool[...] = a
            v32 = pool[pl.ds(0, 160, stride=2), :] + pool[pl.ds(1, 160, stride=2), :]
            total = total + v32.reshape(20, 8, 128).sum(axis=0)
            v = v32.astype(BF16)
            dc[t, r + 1] = v
            grad_line(3 * t, r + 1, v.astype(F32))
            return total

        return lax.fori_loop(0, 4, step, total)

    loads[0].wait()
    bias_total = pool_frame(0, jnp.zeros((8, 128), F32))
    loads[2].wait()
    bias_total = pool_frame(1, bias_total)

    loads[1].wait()

    def stat_step(n, carry):
        s, q = carry
        v = lat[2 + n // 4, 1 + n % 4].astype(F32).reshape(20, 8, 128)
        return s + v.sum(axis=0), q + (v * v).sum(axis=0)

    zero8 = jnp.zeros((8, 128), F32)
    s_sum, q_sum = lax.fori_loop(0, 8, stat_step, (zero8, zero8))
    row8 = lax.broadcasted_iota(jnp.int32, (8, 128), 0)

    def rows_of(*vectors):
        out = zero8
        for n, v in enumerate(vectors):
            out = jnp.where(row8 == n, v.sum(axis=0, keepdims=True), out)
        return out

    st1[h] = rows_of(s_sum, q_sum)

    pl.semaphore_wait(barrier, 13)

    def exchange_start(buf, axis, base):
        me = place[axis]
        out = []
        for d in range(1, size[axis]):
            c = remote(
                buf.at[me], buf.at[me], sm_ss.at[base + d], sm_rs.at[base + d], peer(axis, d)
            )
            c.start()
            out.append(c)
        return out

    def exchange_wait(copies):
        for c in copies:
            c.wait_recv()

    def tile_sum(buf, axis):
        out = buf[0]
        for n in range(1, size[axis]):
            out = out + buf[n]
        return out

    def dc_z(t, part):
        rows = (slice(1, 2), slice(4, 5), slice(2, 4))[part]
        n = 3 * t + part
        return remote(
            dc.at[t, rows],
            dc.at[2 + t, rows],
            dc_ss.at[n],
            dc_rs.at[n],
            {"tm": jnp.maximum(z - 1, 0)},
        )

    def dc_row(f, down):
        n = 6 + 2 * f + down
        src, dst = (4, 0) if down else (1, 5)
        to = {"height": jnp.minimum(h + 1, 7) if down else jnp.maximum(h - 1, 0)}
        return remote(dc.at[f, src], dc.at[f, dst], dc_ss.at[n], dc_rs.at[n], to)

    def lat_z(t, part):
        rows = (slice(1, 2), slice(4, 5), slice(2, 4))[part]
        n = 3 * t + part
        return remote(
            lat.at[2 + t, rows],
            lat.at[t, rows],
            lat_ss.at[n],
            lat_rs.at[n],
            {"tm": jnp.minimum(z + 1, 3)},
        )

    def lat_row(base, down):
        n = 6 + base + down
        src, dst = (4, 0) if down else (1, 5)
        to = {"height": jnp.minimum(h + 1, 7) if down else jnp.maximum(h - 1, 0)}
        return remote(
            lat.at[base : base + 2, src],
            lat.at[base : base + 2, dst],
            lat_ss.at[n],
            lat_rs.at[n],
            to,
        )

    stat_h = exchange_start(st1, "h", 0)

    @pl.when(has_prev)
    def _():
        for part in range(3):
            dc_z(0, part).start()

    @pl.when(has_next)
    def _():
        for part in range(3):
            lat_z(1, part).start()

    for down, there in ((0, has_up), (1, has_down)):

        @pl.when(there)
        def _(down=down):
            dc_row(0, down).start()
            dc_row(1, down).start()

    exchange_wait(stat_h)
    st2[z] = tile_sum(st1, "h")
    stat_z = exchange_start(st2, "z", 8)

    def forward(t):
        @pl.when(has_next)
        def _():
            dc_z(t, 0).wait_recv()
            dc_z(t, 1).wait_recv()
            for down, there in ((0, has_up), (1, has_down)):

                @pl.when(there)
                def _(down=down):
                    dc_row(2 + t, down).start()

    forward(0)

    @pl.when(has_prev)
    def _():
        for part in range(3):
            dc_z(1, part).start()

    @pl.when(has_next)
    def _():
        for part in range(3):
            lat_z(0, part).start()

    for down, there in ((0, has_up), (1, has_down)):

        @pl.when(there)
        def _(down=down):
            lat_row(2, down).start()

    @pl.when(top)
    def _():
        for f in range(4):
            dc[f, 0] = jnp.zeros((160, 128), BF16)

    @pl.when(bottom)
    def _():
        for f in range(4):
            dc[f, 5] = jnp.zeros((160, 128), BF16)

    @pl.when(has_up)
    def _():
        dc_row(0, 1).wait_recv()
        dc_row(1, 1).wait_recv()

    @pl.when(has_down)
    def _():
        dc_row(0, 0).wait_recv()
        dc_row(1, 0).wait_recv()

    def grad_row(slot, f, r):
        grad_line(slot, r, dc[f, r].astype(F32))

    def edge_rows(n, carry):
        grad_row(3 * (n // 2), n // 2, 5 * (n % 2))
        return carry

    lax.fori_loop(0, 4, edge_rows, 0)

    def special_rows(slot):
        @pl.when(top)
        def _():
            dslab[slot, 6] = dslab[slot, 2] + dslab[slot, 1]

        @pl.when(bottom)
        def _():
            dslab[slot, 7] = dslab[slot, 3] + dslab[slot, 4]

    special_rows(0)
    special_rows(3)

    def first_slot(slot, a, b):
        @pl.when(first)
        def _():
            def add(r, carry):
                dslab[slot, r] = dslab[a, r] + dslab[b, r]
                return carry

            lax.fori_loop(0, 6, add, 0)
            special_rows(slot)

    first_slot(1, 0, 3)

    @pl.when(last)
    def _():
        for f in range(2, 4):
            for r in range(6):
                dc[f, r] = jnp.zeros((160, 128), BF16)

    def ahead_inner(t):
        @pl.when(has_next)
        def _():
            dc_z(t, 2).wait_recv()

        def inner(r, carry):
            grad_row(4 + t, 2 + t, r)
            return carry

        lax.fori_loop(1, 5, inner, 0)

    def ahead_outer(t):
        @pl.when(has_next)
        def _():
            @pl.when(has_up)
            def _():
                dc_row(2 + t, 1).wait_recv()

            @pl.when(has_down)
            def _():
                dc_row(2 + t, 0).wait_recv()

        def outer(n, carry):
            grad_row(4 + t, 2 + t, 5 * n)
            return carry

        lax.fori_loop(0, 2, outer, 0)
        special_rows(4 + t)

    ahead_inner(0)

    row_t = jnp.where(top, 6, 2)
    row_b = jnp.where(bottom, 7, 3)

    def taken(slot, j):
        if j == 0:
            parts = [dslab[pl.ds(slot, 1), pl.ds(row_t, 1)][0], dslab[slot, 3:6]]
        elif j == 1:
            parts = [dslab[slot, 1:5]]
        else:
            parts = [dslab[slot, 0:3], dslab[pl.ds(slot, 1), pl.ds(row_b, 1)][0]]
        v = jnp.concatenate(parts, axis=0) if len(parts) > 1 else parts[0]
        return v.reshape(640, 384)

    slot_of = {
        (0, 2): 0,
        (0, 1): jnp.where(first, 1, 3),
        (0, 0): jnp.where(first, 2, 4),
        (1, 2): 3,
        (1, 1): 4,
        (1, 0): 5,
    }

    exchange_wait(stat_z)
    lane_a = lax.broadcasted_iota(jnp.int32, (128, 128), 0) >> 2
    lane_b = lax.broadcasted_iota(jnp.int32, (128, 128), 1) >> 2
    same = jnp.where(lane_a == lane_b, 1.0, 0.0)

    def by_group(v):
        return jnp.dot(v, same, precision=lax.Precision.HIGHEST, preferred_element_type=F32)

    sums = by_group(tile_sum(st2, "z")) / count
    mean = sums[0:1]
    rstd = lax.rsqrt(sums[1:2] - mean * mean + 1e-6)
    for c in loads[4:]:
        c.wait()
    gain = vec[0:1]
    shift = vec[1:2]
    kbias = vec[2:3]

    def normed(f, r):
        return (lat[f, r].astype(F32) - mean) * rstd

    def own_row(f, r, n):
        pre = normed(f, r) * gain + shift
        act_s[pl.ds(pl.multiple_of(n * 160, 160), 160), :] = pre / (1.0 + jnp.exp(-pre))

    def own_rows(n, carry):
        own_row(3 - n // 4, 1 + n % 4, n)
        return carry

    @pl.when(has_prev)
    def _():
        for part in range(3):
            lat_z(1, part).wait_recv()

    lax.fori_loop(0, 12, own_rows, 0)

    def transposed(n, carry):
        rows = pl.ds(pl.multiple_of(n * 128, 128), 128)
        actt[:, rows] = act_s[rows, :].T.astype(BF16)
        return carry

    lax.fori_loop(0, 15, transposed, 0)

    @pl.when(first)
    def _():
        actt[:, 1280:1920] = jnp.zeros((128, 640), BF16)

    def act_line(f, r, a):
        line[8:168, :] = a
        line[7:8, :] = a[0:1]
        line[168:169, :] = a[159:160]
        aslab[f, r, :, 0:128] = line[7:167, :].astype(BF16)
        aslab[f, r, :, 128:256] = a.astype(BF16)
        aslab[f, r, :, 256:384] = line[9:169, :].astype(BF16)

    def act_row(f, r):
        pre = normed(f, r) * gain + shift
        act_line(f, r, pre / (1.0 + jnp.exp(-pre)))

    def weight_grad(i):
        for j in range(3):
            other = taken(3 if i == 0 else slot_of[1, i], j)
            mine = taken(slot_of[0, i], j)
            if i == 0:
                right = jnp.concatenate([mine, other], axis=0)
                left = actt[:, 640:1920]
            else:
                right = jnp.concatenate([other, mine], axis=0)
                left = actt[:, 0:1280]
            part = jnp.dot(left, right, preferred_element_type=F32)
            g[i, :, :, j * 384 : (j + 1) * 384] = part.astype(BF16).reshape(8, 16, 384)

    copies = {}

    def copy_c(i):
        c = remote(
            g.at[i, pl.ds((1 - core) * 4, 4)],
            rc.at[i],
            ar_ss.at[i, 0],
            ar_rs.at[i, 0],
            peer("core", 0),
        )
        c.start()
        copies[i, 0] = [c]

    def reduce_1(i):
        for c in copies[i, 0]:
            c.wait_recv()
        s1[i] = (g[i, pl.ds(core * 4, 4)].astype(F32) + rc[i].astype(F32)).astype(BF16)
        axis = ORDER[i][0]
        me = place[axis]
        copies[i, 1] = []
        for d in range(1, 4):
            c = remote(
                s1.at[i, lax.rem(me + d, 4)],
                r1.at[i, me],
                ar_ss.at[i, d],
                ar_rs.at[i, d],
                peer(axis, d),
            )
            c.start()
            copies[i, 1].append(c)
        r1[i, me] = s1[i, me]

    def exchange(i, step, buf):
        axis = ORDER[i][step - 1]
        me = place[axis]
        copies[i, step] = []
        for d in range(1, 4):
            n = 3 * (step - 1) + d
            c = remote(buf.at[i, me], buf.at[i, me], ar_ss.at[i, n], ar_rs.at[i, n], peer(axis, d))
            c.start()
            copies[i, step].append(c)

    def total_of(buf, i):
        out = buf[i, 0].astype(F32)
        for n in range(1, 4):
            out = out + buf[i, n].astype(F32)
        return out.astype(BF16)

    def reduce_2(i):
        for c in copies[i, 1]:
            c.wait_recv()
        e2[i, place[ORDER[i][1]]] = total_of(r1, i)
        exchange(i, 2, e2)

    def reduce_3(i):
        for c in copies[i, 2]:
            c.wait_recv()
        e3[i, place[ORDER[i][2]]] = total_of(e2, i)
        exchange(i, 3, e3)

    def gather_1(i):
        for c in copies[i, 3]:
            c.wait_recv()
        axis = ORDER[i][0]
        me = core * 4 + place[axis]
        fin[i, me] = total_of(e3, i)
        copies[i, 4] = []
        for d in range(1, 4):
            n = 9 + d
            c = remote(fin.at[i, me], fin.at[i, me], ar_ss.at[i, n], ar_rs.at[i, n], peer(axis, d))
            c.start()
            copies[i, 4].append(c)

    def gather_c(i):
        for c in copies[i, 4]:
            c.wait_recv()
        half = pl.ds(core * 4, 4)
        c = remote(
            fin.at[i, half], fin.at[i, half], ar_ss.at[i, 13], ar_rs.at[i, 13], peer("core", 0)
        )
        c.start()
        copies[i, 5] = [c]

    def finish(i):
        for c in copies[i, 5]:
            c.wait_recv()
        for n in range(9):
            j, k = divmod(n, 3)
            kg[i, j, k * 128 : (k + 1) * 128, :] = (
                fin[i, :, :, n * 128 : (n + 1) * 128].reshape(128, 128).astype(F32)
            )

    weight_grad(2)
    copy_c(2)
    ahead_outer(0)
    first_slot(2, 1, 4)
    weight_grad(1)
    copy_c(1)
    weight_grad(0)
    copy_c(0)

    forward(1)

    @pl.when(has_prev)
    def _():
        lat_z(0, 0).wait_recv()
        lat_z(0, 1).wait_recv()
        for down, there in ((0, has_up), (1, has_down)):

            @pl.when(there)
            def _(down=down):
                lat_row(0, down).start()

        lat_z(0, 2).wait_recv()

    reduce_1(2)
    reduce_1(1)
    loads[3].wait()

    def flip(n, carry):
        i, j = n // 3, n % 3
        for k in range(3):
            kt[i, pl.ds(pl.multiple_of(j * 384 + k * 128, 128), 128), :] = ker[
                i, j, k * 128 : (k + 1) * 128, :
            ].T
        return carry

    lax.fori_loop(0, 9, flip, 0)

    reduce_1(0)
    ahead_inner(1)
    ahead_outer(1)

    def data_grad(p):
        rows = slice(p * 640, (p + 1) * 640)
        for i in (2, 1, 0):
            left = jnp.concatenate([taken(slot_of[p, i], j) for j in range(3)], axis=1)
            part = lax.dot_general(
                left, kt[i], (((1,), (0,)), ((), ())), preferred_element_type=F32
            )
            acc[rows, :] = part if i == 2 else acc[rows, :] + part

    data_grad(0)
    data_grad(1)

    def through(n, carry):
        a, b = carry
        rows = pl.ds(pl.multiple_of(n * 160, 160), 160)
        v = normed(2 + n // 4, 1 + n % 4)
        pre = v * gain + shift
        sig = 1.0 / (1.0 + jnp.exp(-pre))
        d = acc[rows, :] * (sig * (1.0 + pre * (1.0 - sig)))
        acc[rows, :] = d
        xhat_s[rows, :] = v
        b = b + (d * v).reshape(20, 8, 128).sum(axis=0)
        return a + d.reshape(20, 8, 128).sum(axis=0), b

    d_sum, dx_sum = lax.fori_loop(0, 8, through, (zero8, zero8))
    gr1[h] = rows_of(d_sum, dx_sum, bias_total)
    grad_h = exchange_start(gr1, "h", 12)
    for i in (2, 1, 0):
        reduce_2(i)

    @pl.when(top)
    def _():
        for f in range(2, 4):
            lat[f, 0] = lat[f, 1]

    @pl.when(bottom)
    def _():
        for f in range(2, 4):
            lat[f, 5] = lat[f, 4]

    @pl.when(has_up)
    def _():
        lat_row(2, 1).wait_recv()

    @pl.when(has_down)
    def _():
        lat_row(2, 0).wait_recv()

    @pl.when(has_prev)
    def _():
        @pl.when(top)
        def _():
            for f in range(2):
                lat[f, 0] = lat[f, 1]

        @pl.when(bottom)
        def _():
            for f in range(2):
                lat[f, 5] = lat[f, 4]

        @pl.when(has_up)
        def _():
            lat_row(0, 1).wait_recv()

        @pl.when(has_down)
        def _():
            lat_row(0, 0).wait_recv()

    @pl.when(first)
    def _():
        for f in range(2):
            for r in range(6):
                lat[f, r] = lat[2, r]

    def own_lines(n, carry):
        rows = pl.ds(pl.multiple_of(n * 160, 160), 160)
        act_line(3 - n // 4, 1 + n % 4, act_s[rows, :])
        return carry

    lax.fori_loop(0, 8, own_lines, 0)

    def edge_act(n, carry):
        act_row(2 + n // 2, 5 * (n % 2))
        return carry

    lax.fori_loop(0, 4, edge_act, 0)

    def past_act(n, carry):
        act_row(n // 6, n % 6)
        return carry

    lax.fori_loop(0, 12, past_act, 0)
    exchange_wait(grad_h)
    gr2[z] = tile_sum(gr1, "h")
    grad_z = exchange_start(gr2, "z", 20)

    def conv(t):
        rows = slice(t * 640, (t + 1) * 640)
        for i in range(3):
            left = jnp.concatenate(
                [aslab[t + i, j : j + 4].reshape(640, 384) for j in range(3)], axis=1
            )
            part = jnp.dot(left, ker[i].reshape(1152, 128), preferred_element_type=F32)
            cacc[rows, :] = part if i == 0 else cacc[rows, :] + part

        def expand(r, carry):
            v = cacc[pl.ds(pl.multiple_of((t * 4 + r) * 160, 160), 160), :] + kbias
            pool[pl.ds(0, 160, stride=2), :] = v
            pool[pl.ds(1, 160, stride=2), :] = v
            w = pool[...].astype(BF16)
            up[0, t, 2 * r] = w
            up[0, t, 2 * r + 1] = w
            return carry

        lax.fori_loop(0, 4, expand, 0)

    for i in (2, 1, 0):
        reduce_3(i)
    conv(0)
    exchange_wait(grad_z)
    clip_sums = tile_sum(gr2, "z")
    gr3[y] = clip_sums
    grad_y = exchange_start(gr3, "y", 24)

    means = by_group(clip_sums * gain) / count
    mean_a, mean_b = means[0:1], means[1:2]

    def latent_grad(n, carry):
        rows = pl.ds(pl.multiple_of(n * 160, 160), 160)
        v = rstd * (acc[rows, :] * gain - mean_a - xhat_s[rows, :] * mean_b)
        lg[0, n // 4, n % 4] = v.astype(BF16)
        return carry

    lax.fori_loop(0, 8, latent_grad, 0)
    for i in (2, 1, 0):
        gather_1(i)
    conv(1)
    exchange_wait(grad_y)
    small_ref[...] = tile_sum(gr3, "y")
    for i in (2, 1, 0):
        gather_c(i)
    for i in (2, 1, 0):
        finish(i)

    for group in (stat_h, stat_z, grad_h, grad_z, grad_y, *copies.values()):
        for c in group:
            c.wait_send()

    @pl.when(has_prev)
    def _():
        for t in range(2):
            for part in range(3):
                dc_z(t, part).wait_send()

    @pl.when(has_next)
    def _():
        for t in range(2):
            for part in range(3):
                lat_z(t, part).wait_send()

    for down, there in ((0, has_up), (1, has_down)):

        @pl.when(there)
        def _(down=down):
            dc_row(0, down).wait_send()
            dc_row(1, down).wait_send()
            lat_row(2, down).wait_send()

            @pl.when(has_next)
            def _():
                dc_row(2, down).wait_send()
                dc_row(3, down).wait_send()

            @pl.when(has_prev)
            def _():
                lat_row(0, down).wait_send()


def emit(up, lg, kg, small, up_out, lg_out, kg_out, bias_out, gain_out, shift_out, sem):
    copies = [
        pltpu.make_async_copy(src, dst, sem.at[n])
        for n, (src, dst) in enumerate(
            (
                (up, up_out),
                (lg, lg_out),
                (kg, kg_out),
                (small.at[2:3], bias_out),
                (small.at[1:2], gain_out),
                (small.at[0:1], shift_out),
            )
        )
    ]
    for c in copies:
        c.start()
    for c in copies:
        c.wait()


def local(latents, cotangent, gain, bias, kernel, kernel_bias):
    count = 8 * 32 * 160 * (128 // GROUPS)
    hbm = pl.BlockSpec(memory_space=pltpu.HBM)
    vmem = pl.BlockSpec(memory_space=pltpu.VMEM)
    dma = pltpu.SemaphoreType.DMA
    shapes = (
        jax.ShapeDtypeStruct((1, 2, 8, 320, 128), BF16),
        jax.ShapeDtypeStruct((1, 2, 4, 160, 128), BF16),
        jax.ShapeDtypeStruct((3, 3, 384, 128), F32),
    )
    operands = (latents, cotangent, gain[None], bias[None], kernel, kernel_bias[None])
    up, lg, kg, small = pl.pallas_call(
        functools.partial(body, float(count)),
        out_shape=(*shapes, jax.ShapeDtypeStruct((8, 128), F32)),
        in_specs=[hbm] * 6,
        out_specs=(vmem,) * 4,
        scratch_shapes=[
            pltpu.VMEM((8, 128), F32),
            pltpu.VMEM((4, 6, 160, 128), BF16),
            pltpu.VMEM((2, 8, 320, 128), BF16),
            pltpu.VMEM((3, 3, 384, 128), BF16),
            pltpu.VMEM((3, 1152, 128), BF16),
            pltpu.VMEM((4, 6, 160, 128), BF16),
            pltpu.VMEM((6, 8, 160, 384), BF16),
            pltpu.VMEM((4, 6, 160, 384), BF16),
            pltpu.VMEM((176, 128), F32),
            pltpu.VMEM((320, 128), F32),
            pltpu.VMEM((1280, 128), F32),
            pltpu.VMEM((1920, 128), F32),
            pltpu.VMEM((128, 1920), BF16),
            pltpu.VMEM((1280, 128), F32),
            pltpu.VMEM((1280, 128), F32),
            pltpu.VMEM((3, 8, 16, 1152), BF16),
            pltpu.VMEM((3, 4, 16, 1152), BF16),
            pltpu.VMEM((3, 4, 16, 1152), BF16),
            pltpu.VMEM((3, 4, 16, 1152), BF16),
            pltpu.VMEM((3, 4, 16, 1152), BF16),
            pltpu.VMEM((3, 4, 16, 1152), BF16),
            pltpu.VMEM((3, 8, 16, 1152), BF16),
            pltpu.VMEM((8, 8, 128), F32),
            pltpu.VMEM((4, 8, 128), F32),
            pltpu.VMEM((8, 8, 128), F32),
            pltpu.VMEM((4, 8, 128), F32),
            pltpu.VMEM((4, 8, 128), F32),
            dma((7,)),
            dma((10,)),
            dma((10,)),
            dma((14,)),
            dma((14,)),
            dma((28,)),
            dma((28,)),
            dma((3, 14)),
            dma((3, 14)),
        ],
        compiler_params=pltpu.CompilerParams(
            collective_id=0, has_side_effects=True, vmem_limit_bytes=40 * 1024 * 1024
        ),
        cost_estimate=pl.CostEstimate(flops=3 * 2 * 1280 * 3456 * 128, bytes_accessed=6000000, transcendentals=500000),
    )(*(pltpu.with_memory_space_constraint(a, pltpu.HBM) for a in operands))
    row = jax.ShapeDtypeStruct((1, 128), F32)
    up, lg, kg, bias_grad, gain_grad, shift_grad = pl.pallas_call(
        emit,
        out_shape=(*shapes, row, row, row),
        in_specs=[vmem] * 4,
        out_specs=(hbm,) * 6,
        scratch_shapes=[dma((6,))],
        cost_estimate=pl.CostEstimate(flops=0, bytes_accessed=3500000, transcendentals=0),
    )(*(pltpu.with_memory_space_constraint(a, pltpu.VMEM) for a in (up, lg, kg, small)))
    return up, lg, kg, bias_grad[0], gain_grad[0], shift_grad[0]


def solution(mesh):
    split = P("dp", "tm", "height", None, None)
    return jax.shard_map(
        local,
        mesh=mesh,
        in_specs=(split, split, P(), P(), P(), P()),
        out_specs=(split, split, P(), P(), P(), P()),
        check_vma=False,
    )
```

```python
import functools

import jax
import jax.numpy as jnp
from jax import lax
from jax.experimental import pallas as pl
from jax.experimental.pallas import tpu as pltpu
from jax.sharding import PartitionSpec as P

MESH = pl.DeviceIdType.MESH
GROUPS = 32
F32 = jnp.float32
BF16 = jnp.bfloat16

ORDER = {2: ("x", "y", "z"), 1: ("y", "z", "x"), 0: ("z", "x", "y")}


def body(
    count,
    lat_hbm,
    cot_hbm,
    gain_hbm,
    bias_hbm,
    ker_hbm,
    kbias_hbm,
    up,
    lg,
    kg,
    small_ref,
    vec,
    lat,
    cot,
    ker,
    kt,
    dc,
    dslab,
    aslab,
    line,
    pool,
    xhat_s,
    act_s,
    actt,
    pastt,
    acc,
    cacc,
    g,
    rc,
    s1,
    r1,
    e2,
    e3,
    fin,
    st1,
    st2,
    gr1,
    gr2,
    gr3,
    lsem,
    lat_ss,
    lat_rs,
    dc_ss,
    dc_rs,
    sm_ss,
    sm_rs,
    ar_ss,
    ar_rs,
):
    y = lax.axis_index("dp")
    z = lax.axis_index("tm")
    h = lax.axis_index("height")
    x = lax.div(h, 2)
    core = lax.rem(h, 2)
    first, last = z == 0, z == 3
    has_prev, has_next = z > 0, z < 3
    top, bottom = h == 0, h == 7
    has_up, has_down = h > 0, h < 7

    def peer(axis, d):
        if axis == "x":
            return {"height": 2 * lax.rem(x + d, 4) + core}
        if axis == "y":
            return {"dp": lax.rem(y + d, 4)}
        if axis == "z":
            return {"tm": lax.rem(z + d, 4)}
        if axis == "h":
            return {"height": lax.rem(h + d, 8)}
        return {"height": 2 * x + 1 - core}

    place = {"x": x, "y": y, "z": z, "h": h}
    size = {"x": 4, "y": 4, "z": 4, "h": 8}

    def remote(src, dst, ss, rs, to):
        return pltpu.make_async_remote_copy(
            src_ref=src, dst_ref=dst, send_sem=ss, recv_sem=rs, device_id=to, device_id_type=MESH
        )

    loads = [
        pltpu.make_async_copy(lat_hbm.at[0], lat.at[2:4, 1:5], lsem.at[0]),
        pltpu.make_async_copy(cot_hbm.at[0, 0], cot.at[0], lsem.at[1]),
        pltpu.make_async_copy(cot_hbm.at[0, 1], cot.at[1], lsem.at[2]),
        pltpu.make_async_copy(ker_hbm, ker, lsem.at[3]),
        pltpu.make_async_copy(gain_hbm, vec.at[0:1], lsem.at[4]),
        pltpu.make_async_copy(bias_hbm, vec.at[1:2], lsem.at[5]),
        pltpu.make_async_copy(kbias_hbm, vec.at[2:3], lsem.at[6]),
    ]
    for c in loads:
        c.start()

    barrier = pltpu.get_barrier_semaphore()
    greeted = [peer("h", d) for d in range(1, 8)]
    greeted += [peer("z", d) for d in range(1, 4)] + [peer("y", d) for d in range(1, 4)]
    for to in greeted:
        pl.semaphore_signal(barrier, inc=1, device_id=to, device_id_type=MESH)

    row16 = lax.broadcasted_iota(jnp.int32, (16, 128), 0)

    def grad_line(slot, r, v):
        line[8:168, :] = v
        line[7:8, :] = jnp.zeros((1, 128), F32)
        line[168:169, :] = jnp.zeros((1, 128), F32)
        dslab[slot, r, :, 128:256] = v.astype(BF16)
        dslab[slot, r, 16:160, 0:128] = line[25:169, :].astype(BF16)
        dslab[slot, r, 0:16, 0:128] = (
            line[9:25, :] + jnp.where(row16 == 0, v[0:16], 0.0)
        ).astype(BF16)
        dslab[slot, r, 0:144, 256:384] = line[7:151, :].astype(BF16)
        dslab[slot, r, 144:160, 256:384] = (
            line[151:167, :] + jnp.where(row16 == 15, v[144:160], 0.0)
        ).astype(BF16)

    def pool_frame(t, total):
        def step(r, total):
            a = cot[t, 2 * r].astype(F32) + cot[t, 2 * r + 1].astype(F32)
            pool[...] = a
            v32 = pool[pl.ds(0, 160, stride=2), :] + pool[pl.ds(1, 160, stride=2), :]
            total = total + v32.reshape(20, 8, 128).sum(axis=0)
            v = v32.astype(BF16)
            dc[t, r + 1] = v
            grad_line(3 * t, r + 1, v.astype(F32))
            return total

        return lax.fori_loop(0, 4, step, total)

    loads[0].wait()

    def stat_step(n, carry):
        s, q = carry
        v = lat[2 + n // 4, 1 + n % 4].astype(F32).reshape(20, 8, 128)
        return s + v.sum(axis=0), q + (v * v).sum(axis=0)

    zero8 = jnp.zeros((8, 128), F32)
    s_sum, q_sum = lax.fori_loop(0, 8, stat_step, (zero8, zero8))
    row8 = lax.broadcasted_iota(jnp.int32, (8, 128), 0)

    def rows_of(*vectors):
        out = zero8
        for n, v in enumerate(vectors):
            out = jnp.where(row8 == n, v.sum(axis=0, keepdims=True), out)
        return out

    st1[h] = rows_of(s_sum, q_sum)

    pl.semaphore_wait(barrier, 13)

    def exchange_start(buf, axis, base):
        me = place[axis]
        out = []
        for d in range(1, size[axis]):
            c = remote(
                buf.at[me], buf.at[me], sm_ss.at[base + d], sm_rs.at[base + d], peer(axis, d)
            )
            c.start()
            out.append(c)
        return out

    def exchange_wait(copies):
        for c in copies:
            c.wait_recv()

    def tile_sum(buf, axis):
        out = buf[0]
        for n in range(1, size[axis]):
            out = out + buf[n]
        return out

    def dc_z(t, part):
        rows = (slice(1, 2), slice(4, 5), slice(2, 4))[part]
        n = 3 * t + part
        return remote(
            dc.at[t, rows],
            dc.at[2 + t, rows],
            dc_ss.at[n],
            dc_rs.at[n],
            {"tm": jnp.maximum(z - 1, 0)},
        )

    def dc_row(f, down):
        n = 6 + 2 * f + down
        src, dst = (4, 0) if down else (1, 5)
        to = {"height": jnp.minimum(h + 1, 7) if down else jnp.maximum(h - 1, 0)}
        return remote(dc.at[f, src], dc.at[f, dst], dc_ss.at[n], dc_rs.at[n], to)

    def lat_z(t, part):
        rows = (slice(1, 2), slice(4, 5), slice(2, 4))[part]
        n = 3 * t + part
        return remote(
            lat.at[2 + t, rows],
            lat.at[t, rows],
            lat_ss.at[n],
            lat_rs.at[n],
            {"tm": jnp.minimum(z + 1, 3)},
        )

    def lat_row(base, down):
        n = 6 + base + down
        src, dst = (4, 0) if down else (1, 5)
        to = {"height": jnp.minimum(h + 1, 7) if down else jnp.maximum(h - 1, 0)}
        return remote(
            lat.at[base : base + 2, src],
            lat.at[base : base + 2, dst],
            lat_ss.at[n],
            lat_rs.at[n],
            to,
        )

    stat_h = exchange_start(st1, "h", 0)

    @pl.when(has_next)
    def _():
        for part in range(3):
            lat_z(1, part).start()

    for down, there in ((0, has_up), (1, has_down)):

        @pl.when(there)
        def _(down=down):
            lat_row(2, down).start()

    loads[1].wait()
    bias_total = pool_frame(0, zero8)

    @pl.when(has_prev)
    def _():
        for part in range(3):
            dc_z(0, part).start()

    for down, there in ((0, has_up), (1, has_down)):

        @pl.when(there)
        def _(down=down):
            dc_row(0, down).start()

    loads[2].wait()
    bias_total = pool_frame(1, bias_total)

    for down, there in ((0, has_up), (1, has_down)):

        @pl.when(there)
        def _(down=down):
            dc_row(1, down).start()

    exchange_wait(stat_h)
    st2[z] = tile_sum(st1, "h")
    stat_z = exchange_start(st2, "z", 8)

    def forward(t):
        @pl.when(has_next)
        def _():
            dc_z(t, 0).wait_recv()
            dc_z(t, 1).wait_recv()
            for down, there in ((0, has_up), (1, has_down)):

                @pl.when(there)
                def _(down=down):
                    dc_row(2 + t, down).start()

    @pl.when(has_prev)
    def _():
        for part in range(3):
            dc_z(1, part).start()

    @pl.when(has_next)
    def _():
        for part in range(3):
            lat_z(0, part).start()

    @pl.when(top)
    def _():
        for f in range(4):
            dc[f, 0] = jnp.zeros((160, 128), BF16)

    @pl.when(bottom)
    def _():
        for f in range(4):
            dc[f, 5] = jnp.zeros((160, 128), BF16)

    @pl.when(has_up)
    def _():
        dc_row(0, 1).wait_recv()
        dc_row(1, 1).wait_recv()

    @pl.when(has_down)
    def _():
        dc_row(0, 0).wait_recv()
        dc_row(1, 0).wait_recv()

    def grad_row(slot, f, r):
        grad_line(slot, r, dc[f, r].astype(F32))

    def edge_rows(n, carry):
        grad_row(3 * (n // 2), n // 2, 5 * (n % 2))
        return carry

    lax.fori_loop(0, 4, edge_rows, 0)

    def special_rows(slot):
        @pl.when(top)
        def _():
            dslab[slot, 6] = dslab[slot, 2] + dslab[slot, 1]

        @pl.when(bottom)
        def _():
            dslab[slot, 7] = dslab[slot, 3] + dslab[slot, 4]

    special_rows(0)
    special_rows(3)

    def first_slot(slot, a, b, inner):
        @pl.when(first)
        def _():
            def add(n, carry):
                r = n if inner else 5 * n
                dslab[slot, r] = dslab[a, r] + dslab[b, r]
                return carry

            if inner:
                lax.fori_loop(1, 5, add, 0)
            else:
                lax.fori_loop(0, 2, add, 0)
                special_rows(slot)

    first_slot(1, 0, 3, True)

    @pl.when(last)
    def _():
        for f in range(2, 4):
            for r in range(6):
                dc[f, r] = jnp.zeros((160, 128), BF16)

    def ahead_inner(t):
        @pl.when(has_next)
        def _():
            dc_z(t, 2).wait_recv()

        def inner(r, carry):
            grad_row(4 + t, 2 + t, r)
            return carry

        lax.fori_loop(1, 5, inner, 0)

    def ahead_outer(t):
        @pl.when(has_next)
        def _():
            @pl.when(has_up)
            def _():
                dc_row(2 + t, 1).wait_recv()

            @pl.when(has_down)
            def _():
                dc_row(2 + t, 0).wait_recv()

        def outer(n, carry):
            grad_row(4 + t, 2 + t, 5 * n)
            return carry

        lax.fori_loop(0, 2, outer, 0)
        special_rows(4 + t)

    forward(0)
    ahead_inner(0)
    first_slot(2, 1, 4, True)

    @pl.when(top)
    def _():
        for f in range(2, 4):
            lat[f, 0] = lat[f, 1]

    @pl.when(bottom)
    def _():
        for f in range(2, 4):
            lat[f, 5] = lat[f, 4]

    @pl.when(has_up)
    def _():
        lat_row(2, 1).wait_recv()

    @pl.when(has_down)
    def _():
        lat_row(2, 0).wait_recv()

    row_t = jnp.where(top, 6, 2)
    row_b = jnp.where(bottom, 7, 3)

    def taken(slot, j):
        if j == 0:
            parts = [dslab[pl.ds(slot, 1), pl.ds(row_t, 1)][0], dslab[slot, 3:6]]
        elif j == 1:
            parts = [dslab[slot, 1:5]]
        else:
            parts = [dslab[slot, 0:3], dslab[pl.ds(slot, 1), pl.ds(row_b, 1)][0]]
        v = jnp.concatenate(parts, axis=0) if len(parts) > 1 else parts[0]
        return v.reshape(640, 384)

    slot_of = {
        (0, 2): 0,
        (0, 1): jnp.where(first, 1, 3),
        (0, 0): jnp.where(first, 2, 4),
        (1, 2): 3,
        (1, 1): 4,
        (1, 0): 5,
    }

    exchange_wait(stat_z)
    lane_a = lax.broadcasted_iota(jnp.int32, (128, 128), 0) >> 2
    lane_b = lax.broadcasted_iota(jnp.int32, (128, 128), 1) >> 2
    same = jnp.where(lane_a == lane_b, 1.0, 0.0)

    def by_group(v):
        return jnp.dot(v, same, precision=lax.Precision.HIGHEST, preferred_element_type=F32)

    sums = by_group(tile_sum(st2, "z")) / count
    mean = sums[0:1]
    rstd = lax.rsqrt(sums[1:2] - mean * mean + 1e-6)
    for c in loads[4:]:
        c.wait()
    gain = vec[0:1]
    shift = vec[1:2]
    kbias = vec[2:3]

    def normed(f, r):
        return (lat[f, r].astype(F32) - mean) * rstd

    def own_row(f, r, n):
        pre = normed(f, r) * gain + shift
        act_s[pl.ds(pl.multiple_of(n * 160, 160), 160), :] = pre / (1.0 + jnp.exp(-pre))

    def own_rows(n, carry):
        own_row(3 - n // 6, jnp.where(n < 12, n % 6, n - 11), n)
        return carry

    @pl.when(has_prev)
    def _():
        for part in range(3):
            lat_z(1, part).wait_recv()

    lax.fori_loop(0, 16, own_rows, 0)

    eye_a = lax.broadcasted_iota(jnp.int32, (128, 128), 0)
    eye_b = lax.broadcasted_iota(jnp.int32, (128, 128), 1)
    eye = jnp.where(eye_a == eye_b, 1.0, 0.0).astype(BF16)

    def turned(start):
        v = act_s[start : start + 640, :].astype(BF16)
        return lax.dot_general(
            eye, v, (((1,), (1,)), ((), ())), preferred_element_type=F32
        ).astype(BF16)

    for j in range(3):
        for p in range(2):
            actt[j, :, p * 640 : (p + 1) * 640] = turned(p * 960 + j * 160)
    pastt[...] = turned(1920)

    @pl.when(first)
    def _():
        pastt[...] = jnp.zeros((128, 640), BF16)

    def act_line(f, r, a):
        line[8:168, :] = a
        line[7:8, :] = a[0:1]
        line[168:169, :] = a[159:160]
        aslab[f, r, :, 0:128] = line[7:167, :].astype(BF16)
        aslab[f, r, :, 128:256] = a.astype(BF16)
        aslab[f, r, :, 256:384] = line[9:169, :].astype(BF16)

    def act_row(f, r):
        pre = normed(f, r) * gain + shift
        act_line(f, r, pre / (1.0 + jnp.exp(-pre)))

    def weight_grad(i):
        for j in range(3):
            mine = dslab[pl.ds(slot_of[0, i], 1), 1:5].reshape(640, 384)
            if i == 0:
                right = jnp.concatenate([mine, taken(3, j)], axis=0)
                left = jnp.concatenate([actt[j, :, 640:1280], pastt[...]], axis=1)
            else:
                other = dslab[slot_of[1, i], 1:5].reshape(640, 384)
                right = jnp.concatenate([other, mine], axis=0)
                left = actt[j]
            part = jnp.dot(left, right, preferred_element_type=F32)
            g[i, :, :, j * 384 : (j + 1) * 384] = part.reshape(8, 16, 384)

    copies = {}

    def copy_c(i):
        c = remote(
            g.at[i, pl.ds((1 - core) * 4, 4)],
            rc.at[i],
            ar_ss.at[i, 0],
            ar_rs.at[i, 0],
            peer("core", 0),
        )
        c.start()
        copies[i, 0] = [c]

    def reduce_1(i):
        for c in copies[i, 0]:
            c.wait_recv()
        s1[i] = (g[i, pl.ds(core * 4, 4)] + rc[i]).astype(BF16)
        axis = ORDER[i][0]
        me = place[axis]
        copies[i, 1] = []
        for d in range(1, 4):
            c = remote(
                s1.at[i, lax.rem(me + d, 4)],
                r1.at[i, me],
                ar_ss.at[i, d],
                ar_rs.at[i, d],
                peer(axis, d),
            )
            c.start()
            copies[i, 1].append(c)
        r1[i, me] = s1[i, me]

    def exchange(i, step, buf):
        axis = ORDER[i][step - 1]
        me = place[axis]
        copies[i, step] = []
        for d in range(1, 4):
            n = 3 * (step - 1) + d
            c = remote(buf.at[i, me], buf.at[i, me], ar_ss.at[i, n], ar_rs.at[i, n], peer(axis, d))
            c.start()
            copies[i, step].append(c)

    def total_of(buf, i):
        out = buf[i, 0].astype(F32)
        for n in range(1, 4):
            out = out + buf[i, n].astype(F32)
        return out.astype(BF16)

    def reduce_2(i):
        for c in copies[i, 1]:
            c.wait_recv()
        e2[i, place[ORDER[i][1]]] = total_of(r1, i)
        exchange(i, 2, e2)

    def reduce_3(i):
        for c in copies[i, 2]:
            c.wait_recv()
        e3[i, place[ORDER[i][2]]] = total_of(e2, i)
        exchange(i, 3, e3)

    def gather_1(i):
        for c in copies[i, 3]:
            c.wait_recv()
        axis = ORDER[i][0]
        me = core * 4 + place[axis]
        fin[i, me] = total_of(e3, i)
        copies[i, 4] = []
        for d in range(1, 4):
            n = 9 + d
            c = remote(fin.at[i, me], fin.at[i, me], ar_ss.at[i, n], ar_rs.at[i, n], peer(axis, d))
            c.start()
            copies[i, 4].append(c)

    def gather_c(i):
        for c in copies[i, 4]:
            c.wait_recv()
        half = pl.ds(core * 4, 4)
        c = remote(
            fin.at[i, half], fin.at[i, half], ar_ss.at[i, 13], ar_rs.at[i, 13], peer("core", 0)
        )
        c.start()
        copies[i, 5] = [c]

    def finish(i):
        for c in copies[i, 5]:
            c.wait_recv()
        for n in range(9):
            j, k = divmod(n, 3)
            kg[i, j, k * 128 : (k + 1) * 128, :] = (
                fin[i, :, :, n * 128 : (n + 1) * 128].reshape(128, 128).astype(F32)
            )

    weight_grad(2)
    copy_c(2)
    weight_grad(1)
    copy_c(1)
    reduce_1(2)
    forward(1)
    weight_grad(0)
    copy_c(0)
    reduce_1(1)

    @pl.when(has_prev)
    def _():
        lat_z(0, 0).wait_recv()
        lat_z(0, 1).wait_recv()
        for down, there in ((0, has_up), (1, has_down)):

            @pl.when(there)
            def _(down=down):
                lat_row(0, down).start()


    loads[3].wait()

    def flip(n, carry):
        i, j = n // 3, n % 3
        for k in range(3):
            kt[i, pl.ds(pl.multiple_of(j * 384 + k * 128, 128), 128), :] = ker[
                i, j, k * 128 : (k + 1) * 128, :
            ].T
        return carry

    lax.fori_loop(0, 9, flip, 0)

    reduce_1(0)

    def own_lines(n, carry):
        rows = pl.ds(pl.multiple_of(n * 160, 160), 160)
        act_line(3 - n // 6, n % 6, act_s[rows, :])
        return carry

    lax.fori_loop(0, 12, own_lines, 0)

    ahead_inner(1)
    reduce_2(2)
    ahead_outer(0)
    first_slot(1, 0, 3, False)
    first_slot(2, 1, 4, False)
    ahead_outer(1)
    reduce_2(1)
    reduce_2(0)

    def data_grad(p):
        rows = slice(p * 640, (p + 1) * 640)
        for i in (2, 1, 0):
            left = jnp.concatenate([taken(slot_of[p, i], j) for j in range(3)], axis=1)
            part = lax.dot_general(
                left, kt[i], (((1,), (0,)), ((), ())), preferred_element_type=F32
            )
            acc[rows, :] = part if i == 2 else acc[rows, :] + part

    data_grad(0)
    data_grad(1)

    def through(n, carry):
        a, b = carry
        rows = pl.ds(pl.multiple_of(n * 160, 160), 160)
        v = normed(2 + n // 4, 1 + n % 4)
        pre = v * gain + shift
        sig = 1.0 / (1.0 + jnp.exp(-pre))
        d = acc[rows, :] * (sig * (1.0 + pre * (1.0 - sig)))
        acc[rows, :] = d
        xhat_s[rows, :] = v
        b = b + (d * v).reshape(20, 8, 128).sum(axis=0)
        return a + d.reshape(20, 8, 128).sum(axis=0), b

    d_sum, dx_sum = lax.fori_loop(0, 8, through, (zero8, zero8))
    gr1[h] = rows_of(d_sum, dx_sum, bias_total)
    grad_h = exchange_start(gr1, "h", 12)
    for i in (2, 1, 0):
        reduce_3(i)

    @pl.when(has_prev)
    def _():
        lat_z(0, 2).wait_recv()

        @pl.when(top)
        def _():
            for f in range(2):
                lat[f, 0] = lat[f, 1]

        @pl.when(bottom)
        def _():
            for f in range(2):
                lat[f, 5] = lat[f, 4]

        @pl.when(has_up)
        def _():
            lat_row(0, 1).wait_recv()

        @pl.when(has_down)
        def _():
            lat_row(0, 0).wait_recv()

    @pl.when(first)
    def _():
        for f in range(2):
            for r in range(6):
                lat[f, r] = lat[2, r]

    def past_act(n, carry):
        act_row(n // 6, n % 6)
        return carry

    lax.fori_loop(0, 12, past_act, 0)
    def conv(t):
        rows = slice(t * 640, (t + 1) * 640)
        for i in range(3):
            left = jnp.concatenate(
                [aslab[t + i, j : j + 4].reshape(640, 384) for j in range(3)], axis=1
            )
            part = jnp.dot(left, ker[i].reshape(1152, 128), preferred_element_type=F32)
            cacc[rows, :] = part if i == 0 else cacc[rows, :] + part

    def upsample(t):
        def expand(r, carry):
            v = cacc[pl.ds(pl.multiple_of((t * 4 + r) * 160, 160), 160), :] + kbias
            pool[pl.ds(0, 160, stride=2), :] = v
            pool[pl.ds(1, 160, stride=2), :] = v
            w = pool[...].astype(BF16)
            up[0, t, 2 * r] = w
            up[0, t, 2 * r + 1] = w
            return carry

        lax.fori_loop(0, 4, expand, 0)

    conv(0)
    exchange_wait(grad_h)
    gr2[z] = tile_sum(gr1, "h")
    grad_z = exchange_start(gr2, "z", 20)

    for i in (2, 1, 0):
        gather_1(i)
    upsample(0)
    conv(1)
    exchange_wait(grad_z)
    clip_sums = tile_sum(gr2, "z")
    gr3[y] = clip_sums
    grad_y = exchange_start(gr3, "y", 24)

    means = by_group(clip_sums * gain) / count
    mean_a, mean_b = means[0:1], means[1:2]

    def latent_grad(n, carry):
        rows = pl.ds(pl.multiple_of(n * 160, 160), 160)
        v = rstd * (acc[rows, :] * gain - mean_a - xhat_s[rows, :] * mean_b)
        lg[0, n // 4, n % 4] = v.astype(BF16)
        return carry

    lax.fori_loop(0, 8, latent_grad, 0)
    for i in (2, 1, 0):
        gather_c(i)
    upsample(1)
    for i in (2, 1, 0):
        finish(i)
    exchange_wait(grad_y)
    small_ref[...] = tile_sum(gr3, "y")

    for group in (stat_h, stat_z, grad_h, grad_z, grad_y, *copies.values()):
        for c in group:
            c.wait_send()

    @pl.when(has_prev)
    def _():
        for t in range(2):
            for part in range(3):
                dc_z(t, part).wait_send()

    @pl.when(has_next)
    def _():
        for t in range(2):
            for part in range(3):
                lat_z(t, part).wait_send()

    for down, there in ((0, has_up), (1, has_down)):

        @pl.when(there)
        def _(down=down):
            dc_row(0, down).wait_send()
            dc_row(1, down).wait_send()
            lat_row(2, down).wait_send()

            @pl.when(has_next)
            def _():
                dc_row(2, down).wait_send()
                dc_row(3, down).wait_send()

            @pl.when(has_prev)
            def _():
                lat_row(0, down).wait_send()


def emit(up, lg, kg, small, up_out, lg_out, kg_out, bias_out, gain_out, shift_out, sem):
    pairs = [(kg.at[i], kg_out.at[i]) for i in range(3)]
    pairs += [(up.at[0, t], up_out.at[0, t]) for t in range(2)]
    pairs += [
        (lg, lg_out),
        (small.at[2:3], bias_out),
        (small.at[1:2], gain_out),
        (small.at[0:1], shift_out),
    ]
    copies = [
        pltpu.make_async_copy(src, dst, sem.at[n]) for n, (src, dst) in enumerate(pairs)
    ]
    for c in copies:
        c.start()
    for c in copies:
        c.wait()


def local(latents, cotangent, gain, bias, kernel, kernel_bias):
    count = 8 * 32 * 160 * (128 // GROUPS)
    hbm = pl.BlockSpec(memory_space=pltpu.HBM)
    vmem = pl.BlockSpec(memory_space=pltpu.VMEM)
    dma = pltpu.SemaphoreType.DMA
    shapes = (
        jax.ShapeDtypeStruct((1, 2, 8, 320, 128), BF16),
        jax.ShapeDtypeStruct((1, 2, 4, 160, 128), BF16),
        jax.ShapeDtypeStruct((3, 3, 384, 128), F32),
    )
    operands = (latents, cotangent, gain[None], bias[None], kernel, kernel_bias[None])
    up, lg, kg, small = pl.pallas_call(
        functools.partial(body, float(count)),
        out_shape=(*shapes, jax.ShapeDtypeStruct((8, 128), F32)),
        in_specs=[hbm] * 6,
        out_specs=(vmem,) * 4,
        scratch_shapes=[
            pltpu.VMEM((8, 128), F32),
            pltpu.VMEM((4, 6, 160, 128), BF16),
            pltpu.VMEM((2, 8, 320, 128), BF16),
            pltpu.VMEM((3, 3, 384, 128), BF16),
            pltpu.VMEM((3, 1152, 128), BF16),
            pltpu.VMEM((4, 6, 160, 128), BF16),
            pltpu.VMEM((6, 8, 160, 384), BF16),
            pltpu.VMEM((4, 6, 160, 384), BF16),
            pltpu.VMEM((176, 128), F32),
            pltpu.VMEM((320, 128), F32),
            pltpu.VMEM((1280, 128), F32),
            pltpu.VMEM((2560, 128), F32),
            pltpu.VMEM((3, 128, 1280), BF16),
            pltpu.VMEM((128, 640), BF16),
            pltpu.VMEM((1280, 128), F32),
            pltpu.VMEM((1280, 128), F32),
            pltpu.VMEM((3, 8, 16, 1152), F32),
            pltpu.VMEM((3, 4, 16, 1152), F32),
            pltpu.VMEM((3, 4, 16, 1152), BF16),
            pltpu.VMEM((3, 4, 16, 1152), BF16),
            pltpu.VMEM((3, 4, 16, 1152), BF16),
            pltpu.VMEM((3, 4, 16, 1152), BF16),
            pltpu.VMEM((3, 8, 16, 1152), BF16),
            pltpu.VMEM((8, 8, 128), F32),
            pltpu.VMEM((4, 8, 128), F32),
            pltpu.VMEM((8, 8, 128), F32),
            pltpu.VMEM((4, 8, 128), F32),
            pltpu.VMEM((4, 8, 128), F32),
            dma((7,)),
            dma((10,)),
            dma((10,)),
            dma((14,)),
            dma((14,)),
            dma((28,)),
            dma((28,)),
            dma((3, 14)),
            dma((3, 14)),
        ],
        compiler_params=pltpu.CompilerParams(
            collective_id=0, has_side_effects=True, vmem_limit_bytes=40 * 1024 * 1024
        ),
        cost_estimate=pl.CostEstimate(flops=3 * 2 * 1280 * 3456 * 128, bytes_accessed=6000000, transcendentals=500000),
    )(*(pltpu.with_memory_space_constraint(a, pltpu.HBM) for a in operands))
    row = jax.ShapeDtypeStruct((1, 128), F32)
    up, lg, kg, bias_grad, gain_grad, shift_grad = pl.pallas_call(
        emit,
        out_shape=(*shapes, row, row, row),
        in_specs=[vmem] * 4,
        out_specs=(hbm,) * 6,
        scratch_shapes=[dma((9,))],
        cost_estimate=pl.CostEstimate(flops=0, bytes_accessed=3500000, transcendentals=0),
    )(*(pltpu.with_memory_space_constraint(a, pltpu.VMEM) for a in (up, lg, kg, small)))
    return up, lg, kg, bias_grad[0], gain_grad[0], shift_grad[0]


def solution(mesh):
    split = P("dp", "tm", "height", None, None)
    return jax.shard_map(
        local,
        mesh=mesh,
        in_specs=(split, split, P(), P(), P(), P()),
        out_specs=(split, split, P(), P(), P(), P()),
        check_vma=False,
    )
```

```python
import functools

import jax
import jax.numpy as jnp
from jax import lax
from jax.experimental import pallas as pl
from jax.experimental.pallas import tpu as pltpu
from jax.sharding import PartitionSpec as P

MESH = pl.DeviceIdType.MESH
GROUPS = 32
F32 = jnp.float32
BF16 = jnp.bfloat16

ORDER = {2: ("x", "y", "z"), 1: ("y", "z", "x"), 0: ("z", "x", "y")}


def body(
    count,
    lat_hbm,
    cot_hbm,
    gain_hbm,
    bias_hbm,
    ker_hbm,
    kbias_hbm,
    up,
    lg,
    kg,
    small_ref,
    vec,
    lat,
    cot,
    ker,
    kt,
    dc,
    dslab,
    aslab,
    line,
    pool,
    xhat_s,
    act_s,
    actt,
    pastt,
    acc,
    cacc,
    g,
    rc,
    s1,
    r1,
    e2,
    e3,
    fin,
    st1,
    st2,
    gr1,
    gr2,
    gr3,
    lsem,
    lat_ss,
    lat_rs,
    dc_ss,
    dc_rs,
    sm_ss,
    sm_rs,
    ar_ss,
    ar_rs,
):
    y = lax.axis_index("dp")
    z = lax.axis_index("tm")
    h = lax.axis_index("height")
    x = lax.div(h, 2)
    core = lax.rem(h, 2)
    first, last = z == 0, z == 3
    has_prev, has_next = z > 0, z < 3
    top, bottom = h == 0, h == 7
    has_up, has_down = h > 0, h < 7

    def peer(axis, d):
        if axis == "x":
            return {"height": 2 * lax.rem(x + d, 4) + core}
        if axis == "y":
            return {"dp": lax.rem(y + d, 4)}
        if axis == "z":
            return {"tm": lax.rem(z + d, 4)}
        if axis == "h":
            return {"height": lax.rem(h + d, 8)}
        return {"height": 2 * x + 1 - core}

    place = {"x": x, "y": y, "z": z, "h": h}
    size = {"x": 4, "y": 4, "z": 4, "h": 8}

    def remote(src, dst, ss, rs, to):
        return pltpu.make_async_remote_copy(
            src_ref=src, dst_ref=dst, send_sem=ss, recv_sem=rs, device_id=to, device_id_type=MESH
        )

    loads = [
        pltpu.make_async_copy(lat_hbm.at[0], lat.at[2:4, 1:5], lsem.at[0]),
        pltpu.make_async_copy(cot_hbm.at[0, 0], cot.at[0], lsem.at[1]),
        pltpu.make_async_copy(cot_hbm.at[0, 1], cot.at[1], lsem.at[2]),
        pltpu.make_async_copy(ker_hbm, ker, lsem.at[3]),
        pltpu.make_async_copy(gain_hbm, vec.at[0:1], lsem.at[4]),
        pltpu.make_async_copy(bias_hbm, vec.at[1:2], lsem.at[5]),
        pltpu.make_async_copy(kbias_hbm, vec.at[2:3], lsem.at[6]),
    ]
    for c in loads:
        c.start()

    barrier = pltpu.get_barrier_semaphore()
    greeted = [peer("h", d) for d in range(1, 8)]
    greeted += [peer("z", d) for d in range(1, 4)] + [peer("y", d) for d in range(1, 4)]
    for to in greeted:
        pl.semaphore_signal(barrier, inc=1, device_id=to, device_id_type=MESH)

    row16 = lax.broadcasted_iota(jnp.int32, (16, 128), 0)

    def grad_line(slot, r, v):
        line[8:168, :] = v
        line[7:8, :] = jnp.zeros((1, 128), F32)
        line[168:169, :] = jnp.zeros((1, 128), F32)
        dslab[slot, r, :, 128:256] = v.astype(BF16)
        dslab[slot, r, 16:160, 0:128] = line[25:169, :].astype(BF16)
        dslab[slot, r, 0:16, 0:128] = (
            line[9:25, :] + jnp.where(row16 == 0, v[0:16], 0.0)
        ).astype(BF16)
        dslab[slot, r, 0:144, 256:384] = line[7:151, :].astype(BF16)
        dslab[slot, r, 144:160, 256:384] = (
            line[151:167, :] + jnp.where(row16 == 15, v[144:160], 0.0)
        ).astype(BF16)

    def pool_frame(t, total):
        def step(r, total):
            a = cot[t, 2 * r].astype(F32) + cot[t, 2 * r + 1].astype(F32)
            pool[...] = a
            v32 = pool[pl.ds(0, 160, stride=2), :] + pool[pl.ds(1, 160, stride=2), :]
            total = total + v32.reshape(20, 8, 128).sum(axis=0)
            v = v32.astype(BF16)
            dc[t, r + 1] = v
            grad_line(3 * t, r + 1, v.astype(F32))
            return total

        return lax.fori_loop(0, 4, step, total)

    loads[0].wait()

    def stat_step(n, carry):
        s, q = carry
        v = lat[2 + n // 4, 1 + n % 4].astype(F32).reshape(20, 8, 128)
        return s + v.sum(axis=0), q + (v * v).sum(axis=0)

    zero8 = jnp.zeros((8, 128), F32)
    s_sum, q_sum = lax.fori_loop(0, 8, stat_step, (zero8, zero8))
    row8 = lax.broadcasted_iota(jnp.int32, (8, 128), 0)

    def rows_of(*vectors):
        out = zero8
        for n, v in enumerate(vectors):
            out = jnp.where(row8 == n, v.sum(axis=0, keepdims=True), out)
        return out

    st1[h] = rows_of(s_sum, q_sum)

    pl.semaphore_wait(barrier, 13)

    def exchange_start(buf, axis, base):
        me = place[axis]
        out = []
        for d in range(1, size[axis]):
            c = remote(
                buf.at[me], buf.at[me], sm_ss.at[base + d], sm_rs.at[base + d], peer(axis, d)
            )
            c.start()
            out.append(c)
        return out

    def exchange_wait(copies):
        for c in copies:
            c.wait_recv()

    def tile_sum(buf, axis):
        out = buf[0]
        for n in range(1, size[axis]):
            out = out + buf[n]
        return out

    def dc_z(t, part):
        rows = (slice(1, 2), slice(4, 5), slice(2, 4))[part]
        n = 3 * t + part
        return remote(
            dc.at[t, rows],
            dc.at[2 + t, rows],
            dc_ss.at[n],
            dc_rs.at[n],
            {"tm": jnp.maximum(z - 1, 0)},
        )

    def dc_row(f, down):
        n = 6 + 2 * f + down
        src, dst = (4, 0) if down else (1, 5)
        to = {"height": jnp.minimum(h + 1, 7) if down else jnp.maximum(h - 1, 0)}
        return remote(dc.at[f, src], dc.at[f, dst], dc_ss.at[n], dc_rs.at[n], to)

    def lat_z(t, part):
        rows = (slice(1, 2), slice(4, 5), slice(2, 4))[part]
        n = 3 * t + part
        return remote(
            lat.at[2 + t, rows],
            lat.at[t, rows],
            lat_ss.at[n],
            lat_rs.at[n],
            {"tm": jnp.minimum(z + 1, 3)},
        )

    def lat_row(base, down):
        n = 6 + base + down
        src, dst = (4, 0) if down else (1, 5)
        to = {"height": jnp.minimum(h + 1, 7) if down else jnp.maximum(h - 1, 0)}
        return remote(
            lat.at[base : base + 2, src],
            lat.at[base : base + 2, dst],
            lat_ss.at[n],
            lat_rs.at[n],
            to,
        )

    stat_h = exchange_start(st1, "h", 0)

    @pl.when(has_next)
    def _():
        for part in range(3):
            lat_z(1, part).start()

    for down, there in ((0, has_up), (1, has_down)):

        @pl.when(there)
        def _(down=down):
            lat_row(2, down).start()

    loads[1].wait()
    bias_total = pool_frame(0, zero8)

    @pl.when(has_prev)
    def _():
        for part in range(3):
            dc_z(0, part).start()

    for down, there in ((0, has_up), (1, has_down)):

        @pl.when(there)
        def _(down=down):
            dc_row(0, down).start()

    loads[2].wait()
    bias_total = pool_frame(1, bias_total)

    for down, there in ((0, has_up), (1, has_down)):

        @pl.when(there)
        def _(down=down):
            dc_row(1, down).start()

    exchange_wait(stat_h)
    st2[z] = tile_sum(st1, "h")
    stat_z = exchange_start(st2, "z", 8)

    def forward(t):
        @pl.when(has_next)
        def _():
            dc_z(t, 0).wait_recv()
            dc_z(t, 1).wait_recv()
            for down, there in ((0, has_up), (1, has_down)):

                @pl.when(there)
                def _(down=down):
                    dc_row(2 + t, down).start()

    @pl.when(has_prev)
    def _():
        for part in range(3):
            dc_z(1, part).start()

    @pl.when(has_next)
    def _():
        for part in range(3):
            lat_z(0, part).start()

    @pl.when(top)
    def _():
        for f in range(4):
            dc[f, 0] = jnp.zeros((160, 128), BF16)

    @pl.when(bottom)
    def _():
        for f in range(4):
            dc[f, 5] = jnp.zeros((160, 128), BF16)

    @pl.when(has_up)
    def _():
        dc_row(0, 1).wait_recv()
        dc_row(1, 1).wait_recv()

    @pl.when(has_down)
    def _():
        dc_row(0, 0).wait_recv()
        dc_row(1, 0).wait_recv()

    def grad_row(slot, f, r):
        grad_line(slot, r, dc[f, r].astype(F32))

    def edge_rows(n, carry):
        grad_row(3 * (n // 2), n // 2, 5 * (n % 2))
        return carry

    lax.fori_loop(0, 4, edge_rows, 0)

    def special_rows(slot):
        @pl.when(top)
        def _():
            dslab[slot, 6] = dslab[slot, 2] + dslab[slot, 1]

        @pl.when(bottom)
        def _():
            dslab[slot, 7] = dslab[slot, 3] + dslab[slot, 4]

    special_rows(0)
    special_rows(3)

    def first_slot(slot, a, b, inner):
        @pl.when(first)
        def _():
            def add(n, carry):
                r = n if inner else 5 * n
                dslab[slot, r] = dslab[a, r] + dslab[b, r]
                return carry

            if inner:
                lax.fori_loop(1, 5, add, 0)
            else:
                lax.fori_loop(0, 2, add, 0)
                special_rows(slot)

    first_slot(1, 0, 3, True)

    @pl.when(last)
    def _():
        for f in range(2, 4):
            for r in range(6):
                dc[f, r] = jnp.zeros((160, 128), BF16)

    def ahead_inner(t):
        @pl.when(has_next)
        def _():
            dc_z(t, 2).wait_recv()

        def inner(r, carry):
            grad_row(4 + t, 2 + t, r)
            return carry

        lax.fori_loop(1, 5, inner, 0)

    def ahead_outer(t):
        @pl.when(has_next)
        def _():
            @pl.when(has_up)
            def _():
                dc_row(2 + t, 1).wait_recv()

            @pl.when(has_down)
            def _():
                dc_row(2 + t, 0).wait_recv()

        def outer(n, carry):
            grad_row(4 + t, 2 + t, 5 * n)
            return carry

        lax.fori_loop(0, 2, outer, 0)
        special_rows(4 + t)

    forward(0)
    ahead_inner(0)
    first_slot(2, 1, 4, True)

    @pl.when(top)
    def _():
        for f in range(2, 4):
            lat[f, 0] = lat[f, 1]

    @pl.when(bottom)
    def _():
        for f in range(2, 4):
            lat[f, 5] = lat[f, 4]

    @pl.when(has_up)
    def _():
        lat_row(2, 1).wait_recv()

    @pl.when(has_down)
    def _():
        lat_row(2, 0).wait_recv()

    row_t = jnp.where(top, 6, 2)
    row_b = jnp.where(bottom, 7, 3)

    def taken(slot, j):
        if j == 0:
            parts = [dslab[pl.ds(slot, 1), pl.ds(row_t, 1)][0], dslab[slot, 3:6]]
        elif j == 1:
            parts = [dslab[slot, 1:5]]
        else:
            parts = [dslab[slot, 0:3], dslab[pl.ds(slot, 1), pl.ds(row_b, 1)][0]]
        v = jnp.concatenate(parts, axis=0) if len(parts) > 1 else parts[0]
        return v.reshape(640, 384)

    slot_of = {
        (0, 2): 0,
        (0, 1): jnp.where(first, 1, 3),
        (0, 0): jnp.where(first, 2, 4),
        (1, 2): 3,
        (1, 1): 4,
        (1, 0): 5,
    }

    exchange_wait(stat_z)
    lane8 = lax.broadcasted_iota(jnp.int32, (8, 128), 1)

    def by_group(v):
        v = v + pltpu.roll(v, 127, 1)
        v = jnp.where(lane8 % 4 == 0, v + pltpu.roll(v, 126, 1), 0.0)
        v = v + pltpu.roll(v, 1, 1)
        return v + pltpu.roll(v, 2, 1)

    sums = by_group(tile_sum(st2, "z")) / count
    mean = sums[0:1]
    rstd = lax.rsqrt(sums[1:2] - mean * mean + 1e-6)
    for c in loads[4:]:
        c.wait()
    gain = vec[0:1]
    shift = vec[1:2]
    kbias = vec[2:3]

    def normed(f, r):
        return (lat[f, r].astype(F32) - mean) * rstd

    def own_row(f, r, n):
        pre = normed(f, r) * gain + shift
        act_s[pl.ds(pl.multiple_of(n * 160, 160), 160), :] = pre / (1.0 + jnp.exp(-pre))

    def own_rows(n, carry):
        own_row(3 - n // 6, jnp.where(n < 12, n % 6, n - 11), n)
        return carry

    @pl.when(has_prev)
    def _():
        for part in range(3):
            lat_z(1, part).wait_recv()

    lax.fori_loop(0, 16, own_rows, 0)

    eye_a = lax.broadcasted_iota(jnp.int32, (128, 128), 0)
    eye_b = lax.broadcasted_iota(jnp.int32, (128, 128), 1)
    eye = jnp.where(eye_a == eye_b, 1.0, 0.0).astype(BF16)

    def turned(start):
        v = act_s[start : start + 640, :].astype(BF16)
        return lax.dot_general(
            eye, v, (((1,), (1,)), ((), ())), preferred_element_type=F32
        ).astype(BF16)

    for j in range(3):
        for p in range(2):
            actt[j, :, p * 640 : (p + 1) * 640] = turned(p * 960 + j * 160)
    pastt[...] = turned(1920)

    @pl.when(first)
    def _():
        pastt[...] = jnp.zeros((128, 640), BF16)

    def act_line(f, r, a):
        line[8:168, :] = a
        line[7:8, :] = a[0:1]
        line[168:169, :] = a[159:160]
        aslab[f, r, :, 0:128] = line[7:167, :].astype(BF16)
        aslab[f, r, :, 128:256] = a.astype(BF16)
        aslab[f, r, :, 256:384] = line[9:169, :].astype(BF16)

    def act_row(f, r):
        pre = normed(f, r) * gain + shift
        act_line(f, r, pre / (1.0 + jnp.exp(-pre)))

    def weight_grad(i):
        for j in range(3):
            mine = dslab[pl.ds(slot_of[0, i], 1), 1:5].reshape(640, 384)
            if i == 0:
                right = jnp.concatenate([mine, taken(3, j)], axis=0)
                left = jnp.concatenate([actt[j, :, 640:1280], pastt[...]], axis=1)
            else:
                other = dslab[slot_of[1, i], 1:5].reshape(640, 384)
                right = jnp.concatenate([other, mine], axis=0)
                left = actt[j]
            part = jnp.dot(left, right, preferred_element_type=F32)
            g[i, :, :, j * 384 : (j + 1) * 384] = part.reshape(8, 16, 384)

    copies = {}

    def copy_c(i):
        c = remote(
            g.at[i, pl.ds((1 - core) * 4, 4)],
            rc.at[i],
            ar_ss.at[i, 0],
            ar_rs.at[i, 0],
            peer("core", 0),
        )
        c.start()
        copies[i, 0] = [c]

    def reduce_1(i):
        for c in copies[i, 0]:
            c.wait_recv()
        s1[i] = (g[i, pl.ds(core * 4, 4)] + rc[i]).astype(BF16)
        axis = ORDER[i][0]
        me = place[axis]
        copies[i, 1] = []
        for d in range(1, 4):
            c = remote(
                s1.at[i, lax.rem(me + d, 4)],
                r1.at[i, me],
                ar_ss.at[i, d],
                ar_rs.at[i, d],
                peer(axis, d),
            )
            c.start()
            copies[i, 1].append(c)
        r1[i, me] = s1[i, me]

    def exchange(i, step, buf):
        axis = ORDER[i][step - 1]
        me = place[axis]
        copies[i, step] = []
        for d in range(1, 4):
            n = 3 * (step - 1) + d
            c = remote(buf.at[i, me], buf.at[i, me], ar_ss.at[i, n], ar_rs.at[i, n], peer(axis, d))
            c.start()
            copies[i, step].append(c)

    def total_of(buf, i):
        out = buf[i, 0].astype(F32)
        for n in range(1, 4):
            out = out + buf[i, n].astype(F32)
        return out.astype(BF16)

    def reduce_2(i):
        for c in copies[i, 1]:
            c.wait_recv()
        e2[i, place[ORDER[i][1]]] = total_of(r1, i)
        exchange(i, 2, e2)

    def reduce_3(i):
        for c in copies[i, 2]:
            c.wait_recv()
        e3[i, place[ORDER[i][2]]] = total_of(e2, i)
        exchange(i, 3, e3)

    def gather_1(i):
        for c in copies[i, 3]:
            c.wait_recv()
        axis = ORDER[i][0]
        me = core * 4 + place[axis]
        fin[i, me] = total_of(e3, i)
        copies[i, 4] = []
        for d in range(1, 4):
            n = 9 + d
            c = remote(fin.at[i, me], fin.at[i, me], ar_ss.at[i, n], ar_rs.at[i, n], peer(axis, d))
            c.start()
            copies[i, 4].append(c)

    def gather_c(i):
        for c in copies[i, 4]:
            c.wait_recv()
        half = pl.ds(core * 4, 4)
        c = remote(
            fin.at[i, half], fin.at[i, half], ar_ss.at[i, 13], ar_rs.at[i, 13], peer("core", 0)
        )
        c.start()
        copies[i, 5] = [c]

    def finish(i):
        for c in copies[i, 5]:
            c.wait_recv()
        for n in range(9):
            j, k = divmod(n, 3)
            kg[i, j, k * 128 : (k + 1) * 128, :] = (
                fin[i, :, :, n * 128 : (n + 1) * 128].reshape(128, 128).astype(F32)
            )

    weight_grad(2)
    copy_c(2)
    weight_grad(1)
    copy_c(1)
    reduce_1(2)
    forward(1)
    weight_grad(0)
    copy_c(0)
    reduce_1(1)

    @pl.when(has_prev)
    def _():
        lat_z(0, 0).wait_recv()
        lat_z(0, 1).wait_recv()
        for down, there in ((0, has_up), (1, has_down)):

            @pl.when(there)
            def _(down=down):
                lat_row(0, down).start()


    loads[3].wait()

    def flip(n, carry):
        i, j = n // 3, n % 3
        v = lax.dot_general(
            eye, ker[i, j], (((1,), (1,)), ((), ())), preferred_element_type=F32
        ).astype(BF16)
        for k in range(3):
            rows = pl.ds(pl.multiple_of(j * 384 + k * 128, 128), 128)
            kt[i, rows, :] = v[:, k * 128 : (k + 1) * 128]
        return carry

    lax.fori_loop(0, 9, flip, 0)

    reduce_1(0)

    def own_lines(n, carry):
        rows = pl.ds(pl.multiple_of(n * 160, 160), 160)
        act_line(3 - n // 6, n % 6, act_s[rows, :])
        return carry

    lax.fori_loop(0, 12, own_lines, 0)

    ahead_inner(1)
    reduce_2(2)
    ahead_outer(0)
    first_slot(1, 0, 3, False)
    first_slot(2, 1, 4, False)
    ahead_outer(1)
    reduce_2(1)
    reduce_2(0)

    def data_grad(p):
        rows = slice(p * 640, (p + 1) * 640)
        for i in (2, 1, 0):
            left = jnp.concatenate([taken(slot_of[p, i], j) for j in range(3)], axis=1)
            part = lax.dot_general(
                left, kt[i], (((1,), (0,)), ((), ())), preferred_element_type=F32
            )
            acc[rows, :] = part if i == 2 else acc[rows, :] + part

    data_grad(0)
    data_grad(1)

    def through(n, carry):
        a, b = carry
        rows = pl.ds(pl.multiple_of(n * 160, 160), 160)
        v = normed(2 + n // 4, 1 + n % 4)
        pre = v * gain + shift
        sig = 1.0 / (1.0 + jnp.exp(-pre))
        d = acc[rows, :] * (sig * (1.0 + pre * (1.0 - sig)))
        acc[rows, :] = d
        xhat_s[rows, :] = v
        b = b + (d * v).reshape(20, 8, 128).sum(axis=0)
        return a + d.reshape(20, 8, 128).sum(axis=0), b

    d_sum, dx_sum = lax.fori_loop(0, 8, through, (zero8, zero8))
    gr1[h] = rows_of(d_sum, dx_sum, bias_total)
    grad_h = exchange_start(gr1, "h", 12)
    for i in (2, 1, 0):
        reduce_3(i)

    @pl.when(has_prev)
    def _():
        lat_z(0, 2).wait_recv()

        @pl.when(top)
        def _():
            for f in range(2):
                lat[f, 0] = lat[f, 1]

        @pl.when(bottom)
        def _():
            for f in range(2):
                lat[f, 5] = lat[f, 4]

        @pl.when(has_up)
        def _():
            lat_row(0, 1).wait_recv()

        @pl.when(has_down)
        def _():
            lat_row(0, 0).wait_recv()

    @pl.when(first)
    def _():
        for f in range(2):
            for r in range(6):
                lat[f, r] = lat[2, r]

    def past_act(n, carry):
        act_row(n // 6, n % 6)
        return carry

    lax.fori_loop(0, 12, past_act, 0)
    def conv(t):
        rows = slice(t * 640, (t + 1) * 640)
        for i in range(3):
            left = jnp.concatenate(
                [aslab[t + i, j : j + 4].reshape(640, 384) for j in range(3)], axis=1
            )
            part = jnp.dot(left, ker[i].reshape(1152, 128), preferred_element_type=F32)
            cacc[rows, :] = part if i == 0 else cacc[rows, :] + part

    def upsample(t):
        def expand(r, carry):
            v = cacc[pl.ds(pl.multiple_of((t * 4 + r) * 160, 160), 160), :] + kbias
            pool[pl.ds(0, 160, stride=2), :] = v
            pool[pl.ds(1, 160, stride=2), :] = v
            w = pool[...].astype(BF16)
            up[0, t, 2 * r] = w
            up[0, t, 2 * r + 1] = w
            return carry

        lax.fori_loop(0, 4, expand, 0)

    conv(0)
    exchange_wait(grad_h)
    gr2[z] = tile_sum(gr1, "h")
    grad_z = exchange_start(gr2, "z", 20)

    for i in (2, 1, 0):
        gather_1(i)
    upsample(0)
    conv(1)
    exchange_wait(grad_z)
    clip_sums = tile_sum(gr2, "z")
    gr3[y] = clip_sums
    grad_y = exchange_start(gr3, "y", 24)

    means = by_group(clip_sums * gain) / count
    mean_a, mean_b = means[0:1], means[1:2]

    def latent_grad(n, carry):
        rows = pl.ds(pl.multiple_of(n * 160, 160), 160)
        v = rstd * (acc[rows, :] * gain - mean_a - xhat_s[rows, :] * mean_b)
        lg[0, n // 4, n % 4] = v.astype(BF16)
        return carry

    lax.fori_loop(0, 8, latent_grad, 0)
    for i in (2, 1, 0):
        gather_c(i)
    upsample(1)
    for i in (2, 1, 0):
        finish(i)
    exchange_wait(grad_y)
    small_ref[...] = tile_sum(gr3, "y")

    for group in (stat_h, stat_z, grad_h, grad_z, grad_y, *copies.values()):
        for c in group:
            c.wait_send()

    @pl.when(has_prev)
    def _():
        for t in range(2):
            for part in range(3):
                dc_z(t, part).wait_send()

    @pl.when(has_next)
    def _():
        for t in range(2):
            for part in range(3):
                lat_z(t, part).wait_send()

    for down, there in ((0, has_up), (1, has_down)):

        @pl.when(there)
        def _(down=down):
            dc_row(0, down).wait_send()
            dc_row(1, down).wait_send()
            lat_row(2, down).wait_send()

            @pl.when(has_next)
            def _():
                dc_row(2, down).wait_send()
                dc_row(3, down).wait_send()

            @pl.when(has_prev)
            def _():
                lat_row(0, down).wait_send()


def emit(up, lg, kg, small, up_out, lg_out, kg_out, bias_out, gain_out, shift_out, sem):
    pairs = [(kg.at[i], kg_out.at[i]) for i in range(3)]
    pairs += [(up.at[0, t], up_out.at[0, t]) for t in range(2)]
    pairs += [
        (lg, lg_out),
        (small.at[2:3], bias_out),
        (small.at[1:2], gain_out),
        (small.at[0:1], shift_out),
    ]
    copies = [
        pltpu.make_async_copy(src, dst, sem.at[n]) for n, (src, dst) in enumerate(pairs)
    ]
    for c in copies:
        c.start()
    for c in copies:
        c.wait()


def local(latents, cotangent, gain, bias, kernel, kernel_bias):
    count = 8 * 32 * 160 * (128 // GROUPS)
    hbm = pl.BlockSpec(memory_space=pltpu.HBM)
    vmem = pl.BlockSpec(memory_space=pltpu.VMEM)
    dma = pltpu.SemaphoreType.DMA
    shapes = (
        jax.ShapeDtypeStruct((1, 2, 8, 320, 128), BF16),
        jax.ShapeDtypeStruct((1, 2, 4, 160, 128), BF16),
        jax.ShapeDtypeStruct((3, 3, 384, 128), F32),
    )
    operands = (latents, cotangent, gain[None], bias[None], kernel, kernel_bias[None])
    up, lg, kg, small = pl.pallas_call(
        functools.partial(body, float(count)),
        out_shape=(*shapes, jax.ShapeDtypeStruct((8, 128), F32)),
        in_specs=[hbm] * 6,
        out_specs=(vmem,) * 4,
        scratch_shapes=[
            pltpu.VMEM((8, 128), F32),
            pltpu.VMEM((4, 6, 160, 128), BF16),
            pltpu.VMEM((2, 8, 320, 128), BF16),
            pltpu.VMEM((3, 3, 384, 128), BF16),
            pltpu.VMEM((3, 1152, 128), BF16),
            pltpu.VMEM((4, 6, 160, 128), BF16),
            pltpu.VMEM((6, 8, 160, 384), BF16),
            pltpu.VMEM((4, 6, 160, 384), BF16),
            pltpu.VMEM((176, 128), F32),
            pltpu.VMEM((320, 128), F32),
            pltpu.VMEM((1280, 128), F32),
            pltpu.VMEM((2560, 128), F32),
            pltpu.VMEM((3, 128, 1280), BF16),
            pltpu.VMEM((128, 640), BF16),
            pltpu.VMEM((1280, 128), F32),
            pltpu.VMEM((1280, 128), F32),
            pltpu.VMEM((3, 8, 16, 1152), F32),
            pltpu.VMEM((3, 4, 16, 1152), F32),
            pltpu.VMEM((3, 4, 16, 1152), BF16),
            pltpu.VMEM((3, 4, 16, 1152), BF16),
            pltpu.VMEM((3, 4, 16, 1152), BF16),
            pltpu.VMEM((3, 4, 16, 1152), BF16),
            pltpu.VMEM((3, 8, 16, 1152), BF16),
            pltpu.VMEM((8, 8, 128), F32),
            pltpu.VMEM((4, 8, 128), F32),
            pltpu.VMEM((8, 8, 128), F32),
            pltpu.VMEM((4, 8, 128), F32),
            pltpu.VMEM((4, 8, 128), F32),
            dma((7,)),
            dma((10,)),
            dma((10,)),
            dma((14,)),
            dma((14,)),
            dma((28,)),
            dma((28,)),
            dma((3, 14)),
            dma((3, 14)),
        ],
        compiler_params=pltpu.CompilerParams(
            collective_id=0, has_side_effects=True, vmem_limit_bytes=40 * 1024 * 1024
        ),
        cost_estimate=pl.CostEstimate(flops=3 * 2 * 1280 * 3456 * 128, bytes_accessed=6000000, transcendentals=500000),
    )(*(pltpu.with_memory_space_constraint(a, pltpu.HBM) for a in operands))
    row = jax.ShapeDtypeStruct((1, 128), F32)
    up, lg, kg, bias_grad, gain_grad, shift_grad = pl.pallas_call(
        emit,
        out_shape=(*shapes, row, row, row),
        in_specs=[vmem] * 4,
        out_specs=(hbm,) * 6,
        scratch_shapes=[dma((9,))],
        cost_estimate=pl.CostEstimate(flops=0, bytes_accessed=3500000, transcendentals=0),
    )(*(pltpu.with_memory_space_constraint(a, pltpu.VMEM) for a in (up, lg, kg, small)))
    return up, lg, kg, bias_grad[0], gain_grad[0], shift_grad[0]


def solution(mesh):
    split = P("dp", "tm", "height", None, None)
    return jax.shard_map(
        local,
        mesh=mesh,
        in_specs=(split, split, P(), P(), P(), P()),
        out_specs=(split, split, P(), P(), P(), P()),
        check_vma=False,
    )
```

```python
import functools

import jax
import jax.numpy as jnp
from jax import lax
from jax.experimental import pallas as pl
from jax.experimental.pallas import tpu as pltpu
from jax.sharding import PartitionSpec as P

MESH = pl.DeviceIdType.MESH
GROUPS = 32
F32 = jnp.float32
BF16 = jnp.bfloat16

ORDER = {2: ("z", "x", "y"), 1: ("x", "y", "z"), 0: ("y", "z", "x")}


def body(
    count,
    lat_hbm,
    cot_hbm,
    gain_hbm,
    bias_hbm,
    ker_hbm,
    kbias_hbm,
    up,
    lg,
    kg,
    small_ref,
    vec,
    lat,
    cot,
    ker,
    kt,
    dc,
    dslab,
    aslab,
    line,
    pool,
    xhat_s,
    act_s,
    actt,
    pastt,
    acc,
    cacc,
    g,
    rc,
    s1,
    r1,
    e2,
    e3,
    fin,
    st1,
    st2,
    gr1,
    gr2,
    gr3,
    lsem,
    lat_ss,
    lat_rs,
    dc_ss,
    dc_rs,
    sm_ss,
    sm_rs,
    ar_ss,
    ar_rs,
):
    y = lax.axis_index("dp")
    z = lax.axis_index("tm")
    h = lax.axis_index("height")
    x = lax.div(h, 2)
    core = lax.rem(h, 2)
    first, last = z == 0, z == 3
    has_prev, has_next = z > 0, z < 3
    top, bottom = h == 0, h == 7
    has_up, has_down = h > 0, h < 7

    def peer(axis, d):
        if axis == "x":
            return {"height": 2 * lax.rem(x + d, 4) + core}
        if axis == "y":
            return {"dp": lax.rem(y + d, 4)}
        if axis == "z":
            return {"tm": lax.rem(z + d, 4)}
        if axis == "h":
            return {"height": lax.rem(h + d, 8)}
        return {"height": 2 * x + 1 - core}

    place = {"x": x, "y": y, "z": z, "h": h}
    size = {"x": 4, "y": 4, "z": 4, "h": 8}

    def remote(src, dst, ss, rs, to):
        return pltpu.make_async_remote_copy(
            src_ref=src, dst_ref=dst, send_sem=ss, recv_sem=rs, device_id=to, device_id_type=MESH
        )

    loads = [
        pltpu.make_async_copy(lat_hbm.at[0], lat.at[2:4, 1:5], lsem.at[0]),
        pltpu.make_async_copy(cot_hbm.at[0, 0], cot.at[0], lsem.at[1]),
        pltpu.make_async_copy(cot_hbm.at[0, 1], cot.at[1], lsem.at[2]),
        pltpu.make_async_copy(ker_hbm, ker, lsem.at[3]),
        pltpu.make_async_copy(gain_hbm, vec.at[0:1], lsem.at[4]),
        pltpu.make_async_copy(bias_hbm, vec.at[1:2], lsem.at[5]),
        pltpu.make_async_copy(kbias_hbm, vec.at[2:3], lsem.at[6]),
    ]
    loads[0].start()

    barrier = pltpu.get_barrier_semaphore()
    greeted = [peer("h", d) for d in range(1, 8)]
    greeted += [peer("z", d) for d in range(1, 4)] + [peer("y", d) for d in range(1, 4)]
    for to in greeted:
        pl.semaphore_signal(barrier, inc=1, device_id=to, device_id_type=MESH)
    for c in loads[1:]:
        c.start()

    row16 = lax.broadcasted_iota(jnp.int32, (16, 128), 0)

    def grad_line(slot, r, v):
        line[8:168, :] = v
        line[7:8, :] = jnp.zeros((1, 128), F32)
        line[168:169, :] = jnp.zeros((1, 128), F32)
        dslab[slot, r, :, 128:256] = v.astype(BF16)
        dslab[slot, r, 16:160, 0:128] = line[25:169, :].astype(BF16)
        dslab[slot, r, 0:16, 0:128] = (
            line[9:25, :] + jnp.where(row16 == 0, v[0:16], 0.0)
        ).astype(BF16)
        dslab[slot, r, 0:144, 256:384] = line[7:151, :].astype(BF16)
        dslab[slot, r, 144:160, 256:384] = (
            line[151:167, :] + jnp.where(row16 == 15, v[144:160], 0.0)
        ).astype(BF16)

    def pool_frame(t, total):
        def step(r, total):
            a = cot[t, 2 * r].astype(F32) + cot[t, 2 * r + 1].astype(F32)
            pool[...] = a
            v32 = pool[pl.ds(0, 160, stride=2), :] + pool[pl.ds(1, 160, stride=2), :]
            total = total + v32.reshape(20, 8, 128).sum(axis=0)
            v = v32.astype(BF16)
            dc[t, r + 1] = v
            grad_line(3 * t, r + 1, v.astype(F32))
            return total

        return lax.fori_loop(0, 4, step, total)

    loads[0].wait()

    def stat_step(n, carry):
        s, q = carry
        v = lat[2 + n // 4, 1 + n % 4].astype(F32).reshape(20, 8, 128)
        return s + v.sum(axis=0), q + (v * v).sum(axis=0)

    zero8 = jnp.zeros((8, 128), F32)
    s_sum, q_sum = lax.fori_loop(0, 8, stat_step, (zero8, zero8))
    row8 = lax.broadcasted_iota(jnp.int32, (8, 128), 0)

    def rows_of(*vectors):
        out = zero8
        for n, v in enumerate(vectors):
            out = jnp.where(row8 == n, v.sum(axis=0, keepdims=True), out)
        return out

    st1[h] = rows_of(s_sum, q_sum)

    loads[1].wait()
    bias_total = pool_frame(0, zero8)
    loads[2].wait()
    bias_total = pool_frame(1, bias_total)

    pl.semaphore_wait(barrier, 13)

    def exchange_start(buf, axis, base):
        me = place[axis]
        out = []
        for d in range(1, size[axis]):
            c = remote(
                buf.at[me], buf.at[me], sm_ss.at[base + d], sm_rs.at[base + d], peer(axis, d)
            )
            c.start()
            out.append(c)
        return out

    def exchange_wait(copies):
        for c in copies:
            c.wait_recv()

    def tile_sum(buf, axis):
        out = buf[0]
        for n in range(1, size[axis]):
            out = out + buf[n]
        return out

    def dc_z(t, part):
        rows = (slice(1, 2), slice(4, 5), slice(2, 4))[part]
        n = 3 * t + part
        return remote(
            dc.at[t, rows],
            dc.at[2 + t, rows],
            dc_ss.at[n],
            dc_rs.at[n],
            {"tm": jnp.maximum(z - 1, 0)},
        )

    def dc_row(f, down):
        n = 6 + 2 * f + down
        src, dst = (4, 0) if down else (1, 5)
        to = {"height": jnp.minimum(h + 1, 7) if down else jnp.maximum(h - 1, 0)}
        return remote(dc.at[f, src], dc.at[f, dst], dc_ss.at[n], dc_rs.at[n], to)

    def lat_z(t, part):
        rows = (slice(1, 2), slice(4, 5), slice(2, 4))[part]
        n = 3 * t + part
        return remote(
            lat.at[2 + t, rows],
            lat.at[t, rows],
            lat_ss.at[n],
            lat_rs.at[n],
            {"tm": jnp.minimum(z + 1, 3)},
        )

    def lat_row(base, down):
        n = 6 + base + down
        src, dst = (4, 0) if down else (1, 5)
        to = {"height": jnp.minimum(h + 1, 7) if down else jnp.maximum(h - 1, 0)}
        return remote(
            lat.at[base : base + 2, src],
            lat.at[base : base + 2, dst],
            lat_ss.at[n],
            lat_rs.at[n],
            to,
        )

    stat_h = exchange_start(st1, "h", 0)

    @pl.when(has_next)
    def _():
        for part in range(3):
            lat_z(1, part).start()

    for down, there in ((0, has_up), (1, has_down)):

        @pl.when(there)
        def _(down=down):
            lat_row(2, down).start()

    @pl.when(has_prev)
    def _():
        for part in range(3):
            dc_z(0, part).start()

    for down, there in ((0, has_up), (1, has_down)):

        @pl.when(there)
        def _(down=down):
            dc_row(0, down).start()

    for down, there in ((0, has_up), (1, has_down)):

        @pl.when(there)
        def _(down=down):
            dc_row(1, down).start()

    exchange_wait(stat_h)
    st2[z] = tile_sum(st1, "h")
    stat_z = exchange_start(st2, "z", 8)

    def forward(t):
        @pl.when(has_next)
        def _():
            dc_z(t, 0).wait_recv()
            dc_z(t, 1).wait_recv()
            for down, there in ((0, has_up), (1, has_down)):

                @pl.when(there)
                def _(down=down):
                    dc_row(2 + t, down).start()

    @pl.when(has_prev)
    def _():
        for part in range(3):
            dc_z(1, part).start()

    @pl.when(has_next)
    def _():
        for part in range(3):
            lat_z(0, part).start()

    @pl.when(top)
    def _():
        for f in range(4):
            dc[f, 0] = jnp.zeros((160, 128), BF16)

    @pl.when(bottom)
    def _():
        for f in range(4):
            dc[f, 5] = jnp.zeros((160, 128), BF16)

    @pl.when(has_up)
    def _():
        dc_row(0, 1).wait_recv()
        dc_row(1, 1).wait_recv()

    @pl.when(has_down)
    def _():
        dc_row(0, 0).wait_recv()
        dc_row(1, 0).wait_recv()

    def grad_row(slot, f, r):
        grad_line(slot, r, dc[f, r].astype(F32))

    def edge_rows(n, carry):
        grad_row(3 * (n // 2), n // 2, 5 * (n % 2))
        return carry

    lax.fori_loop(0, 4, edge_rows, 0)

    def special_rows(slot):
        @pl.when(top)
        def _():
            dslab[slot, 6] = dslab[slot, 2] + dslab[slot, 1]

        @pl.when(bottom)
        def _():
            dslab[slot, 7] = dslab[slot, 3] + dslab[slot, 4]

    special_rows(0)
    special_rows(3)

    def first_slot(slot, a, b, inner):
        @pl.when(first)
        def _():
            def add(n, carry):
                r = n if inner else 5 * n
                dslab[slot, r] = dslab[a, r] + dslab[b, r]
                return carry

            if inner:
                lax.fori_loop(1, 5, add, 0)
            else:
                lax.fori_loop(0, 2, add, 0)
                special_rows(slot)

    first_slot(1, 0, 3, True)

    @pl.when(last)
    def _():
        for f in range(2, 4):
            for r in range(6):
                dc[f, r] = jnp.zeros((160, 128), BF16)

    def ahead_inner(t):
        @pl.when(has_next)
        def _():
            dc_z(t, 2).wait_recv()

        def inner(r, carry):
            grad_row(4 + t, 2 + t, r)
            return carry

        lax.fori_loop(1, 5, inner, 0)

    def ahead_outer(t):
        @pl.when(has_next)
        def _():
            @pl.when(has_up)
            def _():
                dc_row(2 + t, 1).wait_recv()

            @pl.when(has_down)
            def _():
                dc_row(2 + t, 0).wait_recv()

        def outer(n, carry):
            grad_row(4 + t, 2 + t, 5 * n)
            return carry

        lax.fori_loop(0, 2, outer, 0)
        special_rows(4 + t)

    loads[3].wait()

    def flip(n, carry):
        i, j = n // 3, n % 3
        for k in range(3):
            kt[i, pl.ds(pl.multiple_of(j * 384 + k * 128, 128), 128), :] = ker[
                i, j, k * 128 : (k + 1) * 128, :
            ].T
        return carry

    lax.fori_loop(0, 9, flip, 0)

    forward(0)
    ahead_inner(0)
    first_slot(2, 1, 4, True)

    @pl.when(top)
    def _():
        for f in range(2, 4):
            lat[f, 0] = lat[f, 1]

    @pl.when(bottom)
    def _():
        for f in range(2, 4):
            lat[f, 5] = lat[f, 4]

    @pl.when(has_up)
    def _():
        lat_row(2, 1).wait_recv()

    @pl.when(has_down)
    def _():
        lat_row(2, 0).wait_recv()

    row_t = jnp.where(top, 6, 2)
    row_b = jnp.where(bottom, 7, 3)

    def taken(slot, j):
        if j == 0:
            parts = [dslab[pl.ds(slot, 1), pl.ds(row_t, 1)][0], dslab[slot, 3:6]]
        elif j == 1:
            parts = [dslab[slot, 1:5]]
        else:
            parts = [dslab[slot, 0:3], dslab[pl.ds(slot, 1), pl.ds(row_b, 1)][0]]
        v = jnp.concatenate(parts, axis=0) if len(parts) > 1 else parts[0]
        return v.reshape(640, 384)

    slot_of = {
        (0, 2): 0,
        (0, 1): jnp.where(first, 1, 3),
        (0, 0): jnp.where(first, 2, 4),
        (1, 2): 3,
        (1, 1): 4,
        (1, 0): 5,
    }

    exchange_wait(stat_z)
    lane8 = lax.broadcasted_iota(jnp.int32, (8, 128), 1)

    def by_group(v):
        v = v + pltpu.roll(v, 127, 1)
        v = jnp.where(lane8 % 4 == 0, v + pltpu.roll(v, 126, 1), 0.0)
        v = v + pltpu.roll(v, 1, 1)
        return v + pltpu.roll(v, 2, 1)

    sums = by_group(tile_sum(st2, "z")) / count
    mean = sums[0:1]
    rstd = lax.rsqrt(sums[1:2] - mean * mean + 1e-6)
    for c in loads[4:]:
        c.wait()
    gain = vec[0:1]
    shift = vec[1:2]
    kbias = vec[2:3]

    def normed(f, r):
        return (lat[f, r].astype(F32) - mean) * rstd

    def own_row(f, r, n):
        pre = normed(f, r) * gain + shift
        act_s[pl.ds(pl.multiple_of(n * 160, 160), 160), :] = pre / (1.0 + jnp.exp(-pre))

    def own_rows(n, carry):
        own_row(3 - n // 6, jnp.where(n < 12, n % 6, n - 11), n)
        return carry

    @pl.when(has_prev)
    def _():
        for part in range(3):
            lat_z(1, part).wait_recv()

    lax.fori_loop(0, 16, own_rows, 0)

    eye_a = lax.broadcasted_iota(jnp.int32, (128, 128), 0)
    eye_b = lax.broadcasted_iota(jnp.int32, (128, 128), 1)
    eye = jnp.where(eye_a == eye_b, 1.0, 0.0).astype(BF16)

    def turned(start):
        v = act_s[start : start + 640, :].astype(BF16)
        return lax.dot_general(
            eye, v, (((1,), (1,)), ((), ())), preferred_element_type=F32
        ).astype(BF16)

    for j in range(3):
        for p in range(2):
            actt[j, :, p * 640 : (p + 1) * 640] = turned(p * 960 + j * 160)
    pastt[...] = turned(1920)

    @pl.when(first)
    def _():
        pastt[...] = jnp.zeros((128, 640), BF16)

    def act_line(f, r, a):
        line[8:168, :] = a
        line[7:8, :] = a[0:1]
        line[168:169, :] = a[159:160]
        aslab[f, r, :, 0:128] = line[7:167, :].astype(BF16)
        aslab[f, r, :, 128:256] = a.astype(BF16)
        aslab[f, r, :, 256:384] = line[9:169, :].astype(BF16)

    def act_row(f, r):
        pre = normed(f, r) * gain + shift
        act_line(f, r, pre / (1.0 + jnp.exp(-pre)))

    def own_lines_of(p, i):
        return dslab[pl.ds(slot_of[p, i], 1), 1:5].reshape(640, 384)

    def weight_grad(i):
        if i == 0:
            left = actt[:, :, 640:1280].reshape(384, 640)
            right = own_lines_of(0, 0)
            past = jnp.dot(
                pastt[...],
                jnp.concatenate([taken(3, j) for j in range(3)], axis=1),
                preferred_element_type=F32,
            )
        else:
            left = actt[...].reshape(384, 1280)
            right = jnp.concatenate([own_lines_of(1, i), own_lines_of(0, i)], axis=0)
        part = jnp.dot(left, right, preferred_element_type=F32)
        for j in range(3):
            v = part[j * 128 : (j + 1) * 128]
            if i == 0:
                v = v + past[:, j * 384 : (j + 1) * 384]
            g[i, :, :, j * 384 : (j + 1) * 384] = v.reshape(8, 16, 384)

    copies = {}

    def copy_c(i):
        c = remote(
            g.at[i, pl.ds((1 - core) * 4, 4)],
            rc.at[i],
            ar_ss.at[i, 0],
            ar_rs.at[i, 0],
            peer("core", 0),
        )
        c.start()
        copies[i, 0] = [c]

    def reduce_1(i):
        for c in copies[i, 0]:
            c.wait_recv()
        s1[i] = (g[i, pl.ds(core * 4, 4)] + rc[i]).astype(BF16)
        axis = ORDER[i][0]
        me = place[axis]
        copies[i, 1] = []
        for d in range(1, 4):
            c = remote(
                s1.at[i, lax.rem(me + d, 4)],
                r1.at[i, me],
                ar_ss.at[i, d],
                ar_rs.at[i, d],
                peer(axis, d),
            )
            c.start()
            copies[i, 1].append(c)
        r1[i, me] = s1[i, me]

    def exchange(i, step, buf):
        axis = ORDER[i][step - 1]
        me = place[axis]
        copies[i, step] = []
        for d in range(1, 4):
            n = 3 * (step - 1) + d
            c = remote(buf.at[i, me], buf.at[i, me], ar_ss.at[i, n], ar_rs.at[i, n], peer(axis, d))
            c.start()
            copies[i, step].append(c)

    def total_of(buf, i):
        out = buf[i, 0].astype(F32)
        for n in range(1, 4):
            out = out + buf[i, n].astype(F32)
        return out.astype(BF16)

    def reduce_2(i):
        for c in copies[i, 1]:
            c.wait_recv()
        e2[i, place[ORDER[i][1]]] = total_of(r1, i)
        exchange(i, 2, e2)

    def reduce_3(i):
        for c in copies[i, 2]:
            c.wait_recv()
        e3[i, place[ORDER[i][2]]] = total_of(e2, i)
        exchange(i, 3, e3)

    def gather_1(i):
        for c in copies[i, 3]:
            c.wait_recv()
        axis = ORDER[i][0]
        me = core * 4 + place[axis]
        fin[i, me] = total_of(e3, i)
        copies[i, 4] = []
        for d in range(1, 4):
            n = 9 + d
            c = remote(fin.at[i, me], fin.at[i, me], ar_ss.at[i, n], ar_rs.at[i, n], peer(axis, d))
            c.start()
            copies[i, 4].append(c)

    def gather_c(i):
        for c in copies[i, 4]:
            c.wait_recv()
        half = pl.ds(core * 4, 4)
        c = remote(
            fin.at[i, half], fin.at[i, half], ar_ss.at[i, 13], ar_rs.at[i, 13], peer("core", 0)
        )
        c.start()
        copies[i, 5] = [c]

    def finish(i):
        for c in copies[i, 5]:
            c.wait_recv()
        for n in range(9):
            j, k = divmod(n, 3)
            kg[i, j, k * 128 : (k + 1) * 128, :] = (
                fin[i, :, :, n * 128 : (n + 1) * 128].reshape(128, 128).astype(F32)
            )

    weight_grad(2)
    copy_c(2)
    weight_grad(1)
    copy_c(1)
    reduce_1(2)
    forward(1)
    weight_grad(0)
    copy_c(0)
    reduce_1(1)

    @pl.when(has_prev)
    def _():
        lat_z(0, 0).wait_recv()
        lat_z(0, 1).wait_recv()
        for down, there in ((0, has_up), (1, has_down)):

            @pl.when(there)
            def _(down=down):
                lat_row(0, down).start()


    reduce_1(0)

    def own_lines(n, carry):
        rows = pl.ds(pl.multiple_of(n * 160, 160), 160)
        act_line(3 - n // 6, n % 6, act_s[rows, :])
        return carry

    lax.fori_loop(0, 12, own_lines, 0)

    ahead_inner(1)
    reduce_2(2)
    ahead_outer(0)
    first_slot(1, 0, 3, False)
    first_slot(2, 1, 4, False)
    ahead_outer(1)
    reduce_2(1)
    reduce_2(0)

    def data_grad(p):
        rows = slice(p * 640, (p + 1) * 640)
        for i in (2, 1, 0):
            left = jnp.concatenate([taken(slot_of[p, i], j) for j in range(3)], axis=1)
            part = lax.dot_general(
                left, kt[i], (((1,), (0,)), ((), ())), preferred_element_type=F32
            )
            acc[rows, :] = part if i == 2 else acc[rows, :] + part

    data_grad(0)
    data_grad(1)

    def through(n, carry):
        a, b = carry
        rows = pl.ds(pl.multiple_of(n * 160, 160), 160)
        v = normed(2 + n // 4, 1 + n % 4)
        pre = v * gain + shift
        sig = 1.0 / (1.0 + jnp.exp(-pre))
        d = acc[rows, :] * (sig * (1.0 + pre * (1.0 - sig)))
        acc[rows, :] = d
        xhat_s[rows, :] = v
        b = b + (d * v).reshape(20, 8, 128).sum(axis=0)
        return a + d.reshape(20, 8, 128).sum(axis=0), b

    d_sum, dx_sum = lax.fori_loop(0, 8, through, (zero8, zero8))
    gr1[h] = rows_of(d_sum, dx_sum, bias_total)
    grad_h = exchange_start(gr1, "h", 12)
    for i in (2, 1, 0):
        reduce_3(i)

    @pl.when(has_prev)
    def _():
        lat_z(0, 2).wait_recv()

        @pl.when(top)
        def _():
            for f in range(2):
                lat[f, 0] = lat[f, 1]

        @pl.when(bottom)
        def _():
            for f in range(2):
                lat[f, 5] = lat[f, 4]

        @pl.when(has_up)
        def _():
            lat_row(0, 1).wait_recv()

        @pl.when(has_down)
        def _():
            lat_row(0, 0).wait_recv()

    @pl.when(first)
    def _():
        for f in range(2):
            for r in range(6):
                lat[f, r] = lat[2, r]

    def past_act(n, carry):
        act_row(n // 6, n % 6)
        return carry

    lax.fori_loop(0, 12, past_act, 0)
    def conv(t):
        rows = slice(t * 640, (t + 1) * 640)
        for i in range(3):
            left = jnp.concatenate(
                [aslab[t + i, j : j + 4].reshape(640, 384) for j in range(3)], axis=1
            )
            part = jnp.dot(left, ker[i].reshape(1152, 128), preferred_element_type=F32)
            cacc[rows, :] = part if i == 0 else cacc[rows, :] + part

    def upsample(t):
        def expand(r, carry):
            v = cacc[pl.ds(pl.multiple_of((t * 4 + r) * 160, 160), 160), :] + kbias
            pool[pl.ds(0, 160, stride=2), :] = v
            pool[pl.ds(1, 160, stride=2), :] = v
            w = pool[...].astype(BF16)
            up[0, t, 2 * r] = w
            up[0, t, 2 * r + 1] = w
            return carry

        lax.fori_loop(0, 4, expand, 0)

    conv(0)
    exchange_wait(grad_h)
    gr2[z] = tile_sum(gr1, "h")
    grad_z = exchange_start(gr2, "z", 20)

    for i in (2, 1, 0):
        gather_1(i)
    upsample(0)
    conv(1)
    exchange_wait(grad_z)
    clip_sums = tile_sum(gr2, "z")
    gr3[y] = clip_sums
    grad_y = exchange_start(gr3, "y", 24)

    means = by_group(clip_sums * gain) / count
    mean_a, mean_b = means[0:1], means[1:2]

    def latent_grad(n, carry):
        rows = pl.ds(pl.multiple_of(n * 160, 160), 160)
        v = rstd * (acc[rows, :] * gain - mean_a - xhat_s[rows, :] * mean_b)
        lg[0, n // 4, n % 4] = v.astype(BF16)
        return carry

    lax.fori_loop(0, 8, latent_grad, 0)
    for i in (2, 1, 0):
        gather_c(i)
    upsample(1)
    for i in (2, 1, 0):
        finish(i)
    exchange_wait(grad_y)
    small_ref[...] = tile_sum(gr3, "y")

    for group in (stat_h, stat_z, grad_h, grad_z, grad_y, *copies.values()):
        for c in group:
            c.wait_send()

    @pl.when(has_prev)
    def _():
        for t in range(2):
            for part in range(3):
                dc_z(t, part).wait_send()

    @pl.when(has_next)
    def _():
        for t in range(2):
            for part in range(3):
                lat_z(t, part).wait_send()

    for down, there in ((0, has_up), (1, has_down)):

        @pl.when(there)
        def _(down=down):
            dc_row(0, down).wait_send()
            dc_row(1, down).wait_send()
            lat_row(2, down).wait_send()

            @pl.when(has_next)
            def _():
                dc_row(2, down).wait_send()
                dc_row(3, down).wait_send()

            @pl.when(has_prev)
            def _():
                lat_row(0, down).wait_send()


def emit(up, lg, kg, small, up_out, lg_out, kg_out, bias_out, gain_out, shift_out, sem):
    pairs = [(kg.at[i], kg_out.at[i]) for i in range(3)]
    pairs += [(up.at[0, t], up_out.at[0, t]) for t in range(2)]
    pairs += [
        (lg, lg_out),
        (small.at[2:3], bias_out),
        (small.at[1:2], gain_out),
        (small.at[0:1], shift_out),
    ]
    copies = [
        pltpu.make_async_copy(src, dst, sem.at[n]) for n, (src, dst) in enumerate(pairs)
    ]
    for c in copies:
        c.start()
    for c in copies:
        c.wait()


def local(latents, cotangent, gain, bias, kernel, kernel_bias):
    count = 8 * 32 * 160 * (128 // GROUPS)
    hbm = pl.BlockSpec(memory_space=pltpu.HBM)
    vmem = pl.BlockSpec(memory_space=pltpu.VMEM)
    dma = pltpu.SemaphoreType.DMA
    shapes = (
        jax.ShapeDtypeStruct((1, 2, 8, 320, 128), BF16),
        jax.ShapeDtypeStruct((1, 2, 4, 160, 128), BF16),
        jax.ShapeDtypeStruct((3, 3, 384, 128), F32),
    )
    operands = (latents, cotangent, gain[None], bias[None], kernel, kernel_bias[None])
    up, lg, kg, small = pl.pallas_call(
        functools.partial(body, float(count)),
        out_shape=(*shapes, jax.ShapeDtypeStruct((8, 128), F32)),
        in_specs=[hbm] * 6,
        out_specs=(vmem,) * 4,
        scratch_shapes=[
            pltpu.VMEM((8, 128), F32),
            pltpu.VMEM((4, 6, 160, 128), BF16),
            pltpu.VMEM((2, 8, 320, 128), BF16),
            pltpu.VMEM((3, 3, 384, 128), BF16),
            pltpu.VMEM((3, 1152, 128), BF16),
            pltpu.VMEM((4, 6, 160, 128), BF16),
            pltpu.VMEM((6, 8, 160, 384), BF16),
            pltpu.VMEM((4, 6, 160, 384), BF16),
            pltpu.VMEM((176, 128), F32),
            pltpu.VMEM((320, 128), F32),
            pltpu.VMEM((1280, 128), F32),
            pltpu.VMEM((2560, 128), F32),
            pltpu.VMEM((3, 128, 1280), BF16),
            pltpu.VMEM((128, 640), BF16),
            pltpu.VMEM((1280, 128), F32),
            pltpu.VMEM((1280, 128), F32),
            pltpu.VMEM((3, 8, 16, 1152), F32),
            pltpu.VMEM((3, 4, 16, 1152), F32),
            pltpu.VMEM((3, 4, 16, 1152), BF16),
            pltpu.VMEM((3, 4, 16, 1152), BF16),
            pltpu.VMEM((3, 4, 16, 1152), BF16),
            pltpu.VMEM((3, 4, 16, 1152), BF16),
            pltpu.VMEM((3, 8, 16, 1152), BF16),
            pltpu.VMEM((8, 8, 128), F32),
            pltpu.VMEM((4, 8, 128), F32),
            pltpu.VMEM((8, 8, 128), F32),
            pltpu.VMEM((4, 8, 128), F32),
            pltpu.VMEM((4, 8, 128), F32),
            dma((7,)),
            dma((10,)),
            dma((10,)),
            dma((14,)),
            dma((14,)),
            dma((28,)),
            dma((28,)),
            dma((3, 14)),
            dma((3, 14)),
        ],
        compiler_params=pltpu.CompilerParams(
            collective_id=0, has_side_effects=True, vmem_limit_bytes=40 * 1024 * 1024
        ),
        cost_estimate=pl.CostEstimate(flops=3 * 2 * 1280 * 3456 * 128, bytes_accessed=6000000, transcendentals=500000),
    )(*(pltpu.with_memory_space_constraint(a, pltpu.HBM) for a in operands))
    row = jax.ShapeDtypeStruct((1, 128), F32)
    up, lg, kg, bias_grad, gain_grad, shift_grad = pl.pallas_call(
        emit,
        out_shape=(*shapes, row, row, row),
        in_specs=[vmem] * 4,
        out_specs=(hbm,) * 6,
        scratch_shapes=[dma((9,))],
        cost_estimate=pl.CostEstimate(flops=0, bytes_accessed=3500000, transcendentals=0),
    )(*(pltpu.with_memory_space_constraint(a, pltpu.VMEM) for a in (up, lg, kg, small)))
    return up, lg, kg, bias_grad[0], gain_grad[0], shift_grad[0]


def solution(mesh):
    split = P("dp", "tm", "height", None, None)
    return jax.shard_map(
        local,
        mesh=mesh,
        in_specs=(split, split, P(), P(), P(), P()),
        out_specs=(split, split, P(), P(), P(), P()),
        check_vma=False,
    )
```

```python
import functools

import jax
import jax.numpy as jnp
from jax import lax
from jax.experimental import pallas as pl
from jax.experimental.pallas import tpu as pltpu
from jax.sharding import PartitionSpec as P

MESH = pl.DeviceIdType.MESH
GROUPS = 32
F32 = jnp.float32
BF16 = jnp.bfloat16

ORDER = {2: ("z", "x", "y"), 1: ("x", "y", "z"), 0: ("y", "z", "x")}


def body(
    count,
    lat_hbm,
    cot_hbm,
    gain_hbm,
    bias_hbm,
    ker_hbm,
    kbias_hbm,
    up,
    lg,
    kg,
    small_ref,
    vec,
    lat,
    cot,
    ker,
    kt,
    dc,
    dslab,
    aslab,
    line,
    pool,
    xhat_s,
    act_s,
    actt,
    pastt,
    acc,
    cacc,
    g,
    rc,
    s1,
    r1,
    e2,
    e3,
    fin,
    st1,
    st2,
    gr1,
    gr2,
    gr3,
    lsem,
    lat_ss,
    lat_rs,
    dc_ss,
    dc_rs,
    sm_ss,
    sm_rs,
    ar_ss,
    ar_rs,
):
    y = lax.axis_index("dp")
    z = lax.axis_index("tm")
    h = lax.axis_index("height")
    x = lax.div(h, 2)
    core = lax.rem(h, 2)
    first, last = z == 0, z == 3
    has_prev, has_next = z > 0, z < 3
    top, bottom = h == 0, h == 7
    has_up, has_down = h > 0, h < 7

    def peer(axis, d):
        if axis == "x":
            return {"height": 2 * lax.rem(x + d, 4) + core}
        if axis == "y":
            return {"dp": lax.rem(y + d, 4)}
        if axis == "z":
            return {"tm": lax.rem(z + d, 4)}
        if axis == "h":
            return {"height": lax.rem(h + d, 8)}
        return {"height": 2 * x + 1 - core}

    place = {"x": x, "y": y, "z": z, "h": h}
    size = {"x": 4, "y": 4, "z": 4, "h": 8}

    def remote(src, dst, ss, rs, to):
        return pltpu.make_async_remote_copy(
            src_ref=src, dst_ref=dst, send_sem=ss, recv_sem=rs, device_id=to, device_id_type=MESH
        )

    loads = [
        pltpu.make_async_copy(lat_hbm.at[0], lat.at[2:4, 1:5], lsem.at[0]),
        pltpu.make_async_copy(cot_hbm.at[0, 0], cot.at[0], lsem.at[1]),
        pltpu.make_async_copy(cot_hbm.at[0, 1], cot.at[1], lsem.at[2]),
        pltpu.make_async_copy(ker_hbm, ker, lsem.at[3]),
        pltpu.make_async_copy(gain_hbm, vec.at[0:1], lsem.at[4]),
        pltpu.make_async_copy(bias_hbm, vec.at[1:2], lsem.at[5]),
        pltpu.make_async_copy(kbias_hbm, vec.at[2:3], lsem.at[6]),
    ]
    loads[0].start()

    barrier = pltpu.get_barrier_semaphore()
    greeted = [peer("h", d) for d in range(1, 8)]
    greeted += [peer("z", d) for d in range(1, 4)] + [peer("y", d) for d in range(1, 4)]
    for to in greeted:
        pl.semaphore_signal(barrier, inc=1, device_id=to, device_id_type=MESH)
    for c in loads[1:]:
        c.start()

    row16 = lax.broadcasted_iota(jnp.int32, (16, 128), 0)

    def grad_line(slot, r, v):
        line[8:168, :] = v
        line[7:8, :] = jnp.zeros((1, 128), F32)
        line[168:169, :] = jnp.zeros((1, 128), F32)
        dslab[slot, r, :, 128:256] = v.astype(BF16)
        dslab[slot, r, 16:160, 0:128] = line[25:169, :].astype(BF16)
        dslab[slot, r, 0:16, 0:128] = (
            line[9:25, :] + jnp.where(row16 == 0, v[0:16], 0.0)
        ).astype(BF16)
        dslab[slot, r, 0:144, 256:384] = line[7:151, :].astype(BF16)
        dslab[slot, r, 144:160, 256:384] = (
            line[151:167, :] + jnp.where(row16 == 15, v[144:160], 0.0)
        ).astype(BF16)

    def pool_frame(t, total):
        def step(r, total):
            a = cot[t, 2 * r].astype(F32) + cot[t, 2 * r + 1].astype(F32)
            pool[...] = a
            v32 = pool[pl.ds(0, 160, stride=2), :] + pool[pl.ds(1, 160, stride=2), :]
            total = total + v32.reshape(20, 8, 128).sum(axis=0)
            v = v32.astype(BF16)
            dc[t, r + 1] = v
            grad_line(3 * t, r + 1, v.astype(F32))
            return total

        return lax.fori_loop(0, 4, step, total)

    loads[0].wait()

    def stat_step(n, carry):
        s, q = carry
        v = lat[2 + n // 4, 1 + n % 4].astype(F32).reshape(20, 8, 128)
        return s + v.sum(axis=0), q + (v * v).sum(axis=0)

    zero8 = jnp.zeros((8, 128), F32)
    s_sum, q_sum = lax.fori_loop(0, 8, stat_step, (zero8, zero8))
    row8 = lax.broadcasted_iota(jnp.int32, (8, 128), 0)

    def rows_of(*vectors):
        out = zero8
        for n, v in enumerate(vectors):
            out = jnp.where(row8 == n, v.sum(axis=0, keepdims=True), out)
        return out

    st1[h] = rows_of(s_sum, q_sum)

    loads[1].wait()
    bias_total = pool_frame(0, zero8)
    loads[2].wait()
    bias_total = pool_frame(1, bias_total)

    pl.semaphore_wait(barrier, 13)

    def exchange_start(buf, axis, base):
        me = place[axis]
        out = []
        for d in range(1, size[axis]):
            c = remote(
                buf.at[me], buf.at[me], sm_ss.at[base + d], sm_rs.at[base + d], peer(axis, d)
            )
            c.start()
            out.append(c)
        return out

    def exchange_wait(copies):
        for c in copies:
            c.wait_recv()

    def tile_sum(buf, axis):
        out = buf[0]
        for n in range(1, size[axis]):
            out = out + buf[n]
        return out

    def dc_z(t, part):
        rows = (slice(1, 2), slice(4, 5), slice(2, 4))[part]
        n = 3 * t + part
        return remote(
            dc.at[t, rows],
            dc.at[2 + t, rows],
            dc_ss.at[n],
            dc_rs.at[n],
            {"tm": jnp.maximum(z - 1, 0)},
        )

    def dc_row(f, down):
        n = 6 + 2 * f + down
        src, dst = (4, 0) if down else (1, 5)
        to = {"height": jnp.minimum(h + 1, 7) if down else jnp.maximum(h - 1, 0)}
        return remote(dc.at[f, src], dc.at[f, dst], dc_ss.at[n], dc_rs.at[n], to)

    def lat_z(t, part):
        rows = (slice(1, 2), slice(4, 5), slice(2, 4))[part]
        n = 3 * t + part
        return remote(
            lat.at[2 + t, rows],
            lat.at[t, rows],
            lat_ss.at[n],
            lat_rs.at[n],
            {"tm": jnp.minimum(z + 1, 3)},
        )

    def lat_row(base, down):
        n = 6 + base + down
        src, dst = (4, 0) if down else (1, 5)
        to = {"height": jnp.minimum(h + 1, 7) if down else jnp.maximum(h - 1, 0)}
        return remote(
            lat.at[base : base + 2, src],
            lat.at[base : base + 2, dst],
            lat_ss.at[n],
            lat_rs.at[n],
            to,
        )

    stat_h = exchange_start(st1, "h", 0)

    @pl.when(has_next)
    def _():
        for part in range(3):
            lat_z(1, part).start()

    for down, there in ((0, has_up), (1, has_down)):

        @pl.when(there)
        def _(down=down):
            lat_row(2, down).start()

    @pl.when(has_prev)
    def _():
        for part in range(3):
            dc_z(0, part).start()

    for down, there in ((0, has_up), (1, has_down)):

        @pl.when(there)
        def _(down=down):
            dc_row(0, down).start()

    for down, there in ((0, has_up), (1, has_down)):

        @pl.when(there)
        def _(down=down):
            dc_row(1, down).start()

    exchange_wait(stat_h)
    st2[z] = tile_sum(st1, "h")
    stat_z = exchange_start(st2, "z", 8)

    def forward(t):
        @pl.when(has_next)
        def _():
            dc_z(t, 0).wait_recv()
            dc_z(t, 1).wait_recv()
            for down, there in ((0, has_up), (1, has_down)):

                @pl.when(there)
                def _(down=down):
                    dc_row(2 + t, down).start()

    @pl.when(has_prev)
    def _():
        for part in range(3):
            dc_z(1, part).start()

    @pl.when(has_next)
    def _():
        for part in range(3):
            lat_z(0, part).start()

    @pl.when(top)
    def _():
        for f in range(4):
            dc[f, 0] = jnp.zeros((160, 128), BF16)

    @pl.when(bottom)
    def _():
        for f in range(4):
            dc[f, 5] = jnp.zeros((160, 128), BF16)

    @pl.when(has_up)
    def _():
        dc_row(0, 1).wait_recv()
        dc_row(1, 1).wait_recv()

    @pl.when(has_down)
    def _():
        dc_row(0, 0).wait_recv()
        dc_row(1, 0).wait_recv()

    def grad_row(slot, f, r):
        grad_line(slot, r, dc[f, r].astype(F32))

    def edge_rows(n, carry):
        grad_row(3 * (n // 2), n // 2, 5 * (n % 2))
        return carry

    lax.fori_loop(0, 4, edge_rows, 0)

    def special_rows(slot):
        @pl.when(top)
        def _():
            dslab[slot, 6] = dslab[slot, 2] + dslab[slot, 1]

        @pl.when(bottom)
        def _():
            dslab[slot, 7] = dslab[slot, 3] + dslab[slot, 4]

    special_rows(0)
    special_rows(3)

    def first_slot(slot, a, b, inner):
        @pl.when(first)
        def _():
            def add(n, carry):
                r = n if inner else 5 * n
                dslab[slot, r] = dslab[a, r] + dslab[b, r]
                return carry

            if inner:
                lax.fori_loop(1, 5, add, 0)
            else:
                lax.fori_loop(0, 2, add, 0)
                special_rows(slot)

    first_slot(1, 0, 3, True)

    @pl.when(last)
    def _():
        for f in range(2, 4):
            for r in range(6):
                dc[f, r] = jnp.zeros((160, 128), BF16)

    def ahead_inner(t):
        @pl.when(has_next)
        def _():
            dc_z(t, 2).wait_recv()

        def inner(r, carry):
            grad_row(4 + t, 2 + t, r)
            return carry

        lax.fori_loop(1, 5, inner, 0)

    def ahead_outer(t):
        @pl.when(has_next)
        def _():
            @pl.when(has_up)
            def _():
                dc_row(2 + t, 1).wait_recv()

            @pl.when(has_down)
            def _():
                dc_row(2 + t, 0).wait_recv()

        def outer(n, carry):
            grad_row(4 + t, 2 + t, 5 * n)
            return carry

        lax.fori_loop(0, 2, outer, 0)
        special_rows(4 + t)

    loads[3].wait()

    def flip(n, carry):
        i, j = n // 3, n % 3
        for k in range(3):
            kt[i, pl.ds(pl.multiple_of(j * 384 + k * 128, 128), 128), :] = ker[
                i, j, k * 128 : (k + 1) * 128, :
            ].T
        return carry

    lax.fori_loop(0, 9, flip, 0)

    forward(0)
    ahead_inner(0)
    first_slot(2, 1, 4, True)

    @pl.when(top)
    def _():
        for f in range(2, 4):
            lat[f, 0] = lat[f, 1]

    @pl.when(bottom)
    def _():
        for f in range(2, 4):
            lat[f, 5] = lat[f, 4]

    @pl.when(has_up)
    def _():
        lat_row(2, 1).wait_recv()

    @pl.when(has_down)
    def _():
        lat_row(2, 0).wait_recv()

    row_t = jnp.where(top, 6, 2)
    row_b = jnp.where(bottom, 7, 3)

    def taken(slot, j):
        if j == 0:
            parts = [dslab[pl.ds(slot, 1), pl.ds(row_t, 1)][0], dslab[slot, 3:6]]
        elif j == 1:
            parts = [dslab[slot, 1:5]]
        else:
            parts = [dslab[slot, 0:3], dslab[pl.ds(slot, 1), pl.ds(row_b, 1)][0]]
        v = jnp.concatenate(parts, axis=0) if len(parts) > 1 else parts[0]
        return v.reshape(640, 384)

    slot_of = {
        (0, 2): 0,
        (0, 1): jnp.where(first, 1, 3),
        (0, 0): jnp.where(first, 2, 4),
        (1, 2): 3,
        (1, 1): 4,
        (1, 0): 5,
    }

    exchange_wait(stat_z)
    lane8 = lax.broadcasted_iota(jnp.int32, (8, 128), 1)

    def by_group(v):
        v = v + pltpu.roll(v, 127, 1)
        v = jnp.where(lane8 % 4 == 0, v + pltpu.roll(v, 126, 1), 0.0)
        v = v + pltpu.roll(v, 1, 1)
        return v + pltpu.roll(v, 2, 1)

    sums = by_group(tile_sum(st2, "z")) / count
    mean = sums[0:1]
    rstd = lax.rsqrt(sums[1:2] - mean * mean + 1e-6)
    for c in loads[4:]:
        c.wait()
    gain = vec[0:1]
    shift = vec[1:2]
    kbias = vec[2:3]

    def normed(f, r):
        return (lat[f, r].astype(F32) - mean) * rstd

    def own_row(f, r, n):
        pre = normed(f, r) * gain + shift
        act_s[pl.ds(pl.multiple_of(n * 160, 160), 160), :] = pre / (1.0 + jnp.exp(-pre))

    def own_rows(n, carry):
        own_row(3 - n // 6, jnp.where(n < 12, n % 6, n - 11), n)
        return carry

    @pl.when(has_prev)
    def _():
        for part in range(3):
            lat_z(1, part).wait_recv()

    lax.fori_loop(0, 16, own_rows, 0)

    eye_a = lax.broadcasted_iota(jnp.int32, (128, 128), 0)
    eye_b = lax.broadcasted_iota(jnp.int32, (128, 128), 1)
    eye = jnp.where(eye_a == eye_b, 1.0, 0.0).astype(BF16)

    def turned(start):
        v = act_s[start : start + 640, :].astype(BF16)
        return lax.dot_general(
            eye, v, (((1,), (1,)), ((), ())), preferred_element_type=F32
        ).astype(BF16)

    for j in range(3):
        for p in range(2):
            actt[j, :, p * 640 : (p + 1) * 640] = turned(p * 960 + j * 160)
    pastt[...] = turned(1920)

    @pl.when(first)
    def _():
        pastt[...] = jnp.zeros((128, 640), BF16)

    def act_line(f, r, a):
        line[8:168, :] = a
        line[7:8, :] = a[0:1]
        line[168:169, :] = a[159:160]
        aslab[f, r, :, 0:128] = line[7:167, :].astype(BF16)
        aslab[f, r, :, 128:256] = a.astype(BF16)
        aslab[f, r, :, 256:384] = line[9:169, :].astype(BF16)

    def act_row(f, r):
        pre = normed(f, r) * gain + shift
        act_line(f, r, pre / (1.0 + jnp.exp(-pre)))

    def own_lines_of(p, i):
        return dslab[pl.ds(slot_of[p, i], 1), 1:5].reshape(640, 384)

    def weight_grad(i):
        if i == 0:
            left = actt[:, :, 640:1280].reshape(384, 640)
            right = own_lines_of(0, 0)
            past = jnp.dot(
                pastt[...],
                jnp.concatenate([taken(3, j) for j in range(3)], axis=1),
                preferred_element_type=F32,
            )
        else:
            left = actt[...].reshape(384, 1280)
            right = jnp.concatenate([own_lines_of(1, i), own_lines_of(0, i)], axis=0)
        part = jnp.dot(left, right, preferred_element_type=F32)
        for j in range(3):
            v = part[j * 128 : (j + 1) * 128]
            if i == 0:
                v = v + past[:, j * 384 : (j + 1) * 384]
            g[i, :, :, j * 384 : (j + 1) * 384] = v.reshape(8, 16, 384)

    copies = {}

    def copy_c(i):
        c = remote(
            g.at[i, pl.ds((1 - core) * 4, 4)],
            rc.at[i],
            ar_ss.at[i, 0],
            ar_rs.at[i, 0],
            peer("core", 0),
        )
        c.start()
        copies[i, 0] = [c]

    def reduce_1(i):
        for c in copies[i, 0]:
            c.wait_recv()
        s1[i] = (g[i, pl.ds(core * 4, 4)] + rc[i]).astype(BF16)
        axis = ORDER[i][0]
        me = place[axis]
        copies[i, 1] = []
        for d in range(1, 4):
            c = remote(
                s1.at[i, lax.rem(me + d, 4)],
                r1.at[i, me],
                ar_ss.at[i, d],
                ar_rs.at[i, d],
                peer(axis, d),
            )
            c.start()
            copies[i, 1].append(c)
        r1[i, me] = s1[i, me]

    def exchange(i, step, buf):
        axis = ORDER[i][step - 1]
        me = place[axis]
        copies[i, step] = []
        for d in range(1, 4):
            n = 3 * (step - 1) + d
            c = remote(buf.at[i, me], buf.at[i, me], ar_ss.at[i, n], ar_rs.at[i, n], peer(axis, d))
            c.start()
            copies[i, step].append(c)

    def total_of(buf, i):
        out = buf[i, 0].astype(F32)
        for n in range(1, 4):
            out = out + buf[i, n].astype(F32)
        return out.astype(BF16)

    def reduce_2(i):
        for c in copies[i, 1]:
            c.wait_recv()
        e2[i, place[ORDER[i][1]]] = total_of(r1, i)
        exchange(i, 2, e2)

    def reduce_3(i):
        for c in copies[i, 2]:
            c.wait_recv()
        e3[i, place[ORDER[i][2]]] = total_of(e2, i)
        exchange(i, 3, e3)

    def gather_1(i):
        for c in copies[i, 3]:
            c.wait_recv()
        axis = ORDER[i][0]
        me = core * 4 + place[axis]
        fin[i, me] = total_of(e3, i)
        copies[i, 4] = []
        copies[i, 5] = []
        for d in range(1, 4):
            n = 9 + d
            c = remote(fin.at[i, me], fin.at[i, me], ar_ss.at[i, n], ar_rs.at[i, n], peer(axis, d))
            c.start()
            copies[i, 4].append(c)
        to_core(i, me, 0)

    def to_core(i, block, d):
        c = remote(
            fin.at[i, block],
            fin.at[i, block],
            ar_ss.at[i, 13 + d],
            ar_rs.at[i, 13 + d],
            peer("core", 0),
        )
        c.start()
        copies[i, 5].append(c)

    def gather_c(i):
        here = place[ORDER[i][0]]
        for d in (3, 1, 2):
            copies[i, 4][d - 1].wait_recv()
            to_core(i, core * 4 + lax.rem(here - d + 4, 4), d)

    def finish(i):
        for c in copies[i, 5]:
            c.wait_recv()
        for n in range(9):
            j, k = divmod(n, 3)
            kg[i, j, k * 128 : (k + 1) * 128, :] = (
                fin[i, :, :, n * 128 : (n + 1) * 128].reshape(128, 128).astype(F32)
            )

    weight_grad(2)
    copy_c(2)
    weight_grad(1)
    copy_c(1)
    reduce_1(2)
    forward(1)
    weight_grad(0)
    copy_c(0)
    reduce_1(1)

    @pl.when(has_prev)
    def _():
        lat_z(0, 0).wait_recv()
        lat_z(0, 1).wait_recv()
        for down, there in ((0, has_up), (1, has_down)):

            @pl.when(there)
            def _(down=down):
                lat_row(0, down).start()


    reduce_1(0)

    def own_lines(n, carry):
        rows = pl.ds(pl.multiple_of(n * 160, 160), 160)
        act_line(3 - n // 6, n % 6, act_s[rows, :])
        return carry

    lax.fori_loop(0, 12, own_lines, 0)

    ahead_inner(1)
    reduce_2(2)
    ahead_outer(0)
    first_slot(1, 0, 3, False)
    first_slot(2, 1, 4, False)
    ahead_outer(1)
    reduce_2(1)
    reduce_2(0)

    def data_grad(p):
        rows = slice(p * 640, (p + 1) * 640)
        for i in (2, 1, 0):
            left = jnp.concatenate([taken(slot_of[p, i], j) for j in range(3)], axis=1)
            part = lax.dot_general(
                left, kt[i], (((1,), (0,)), ((), ())), preferred_element_type=F32
            )
            acc[rows, :] = part if i == 2 else acc[rows, :] + part

    data_grad(0)
    data_grad(1)

    def through(n, carry):
        a, b = carry
        rows = pl.ds(pl.multiple_of(n * 160, 160), 160)
        v = normed(2 + n // 4, 1 + n % 4)
        pre = v * gain + shift
        sig = 1.0 / (1.0 + jnp.exp(-pre))
        d = acc[rows, :] * (sig * (1.0 + pre * (1.0 - sig)))
        acc[rows, :] = d
        xhat_s[rows, :] = v
        b = b + (d * v).reshape(20, 8, 128).sum(axis=0)
        return a + d.reshape(20, 8, 128).sum(axis=0), b

    d_sum, dx_sum = lax.fori_loop(0, 8, through, (zero8, zero8))
    gr1[h] = rows_of(d_sum, dx_sum, bias_total)
    grad_h = exchange_start(gr1, "h", 12)
    for i in (2, 1, 0):
        reduce_3(i)

    @pl.when(has_prev)
    def _():
        lat_z(0, 2).wait_recv()

        @pl.when(top)
        def _():
            for f in range(2):
                lat[f, 0] = lat[f, 1]

        @pl.when(bottom)
        def _():
            for f in range(2):
                lat[f, 5] = lat[f, 4]

        @pl.when(has_up)
        def _():
            lat_row(0, 1).wait_recv()

        @pl.when(has_down)
        def _():
            lat_row(0, 0).wait_recv()

    @pl.when(first)
    def _():
        for f in range(2):
            for r in range(6):
                lat[f, r] = lat[2, r]

    def past_act(n, carry):
        act_row(n // 6, n % 6)
        return carry

    lax.fori_loop(0, 12, past_act, 0)
    def conv(t):
        rows = slice(t * 640, (t + 1) * 640)
        for i in range(3):
            left = jnp.concatenate(
                [aslab[t + i, j : j + 4].reshape(640, 384) for j in range(3)], axis=1
            )
            part = jnp.dot(left, ker[i].reshape(1152, 128), preferred_element_type=F32)
            cacc[rows, :] = part if i == 0 else cacc[rows, :] + part

    def upsample(t):
        def expand(r, carry):
            v = cacc[pl.ds(pl.multiple_of((t * 4 + r) * 160, 160), 160), :] + kbias
            pool[pl.ds(0, 160, stride=2), :] = v
            pool[pl.ds(1, 160, stride=2), :] = v
            w = pool[...].astype(BF16)
            up[0, t, 2 * r] = w
            up[0, t, 2 * r + 1] = w
            return carry

        lax.fori_loop(0, 4, expand, 0)

    conv(0)
    exchange_wait(grad_h)
    gr2[z] = tile_sum(gr1, "h")
    grad_z = exchange_start(gr2, "z", 20)

    for i in (2, 1, 0):
        gather_1(i)
    upsample(0)
    conv(1)
    exchange_wait(grad_z)
    clip_sums = tile_sum(gr2, "z")
    gr3[y] = clip_sums
    grad_y = exchange_start(gr3, "y", 24)

    means = by_group(clip_sums * gain) / count
    mean_a, mean_b = means[0:1], means[1:2]

    def latent_grad(n, carry):
        rows = pl.ds(pl.multiple_of(n * 160, 160), 160)
        v = rstd * (acc[rows, :] * gain - mean_a - xhat_s[rows, :] * mean_b)
        lg[0, n // 4, n % 4] = v.astype(BF16)
        return carry

    lax.fori_loop(0, 8, latent_grad, 0)
    for i in (2, 1, 0):
        gather_c(i)
    upsample(1)
    for i in (2, 1, 0):
        finish(i)
    exchange_wait(grad_y)
    small_ref[...] = tile_sum(gr3, "y")

    for group in (stat_h, stat_z, grad_h, grad_z, grad_y, *copies.values()):
        for c in group:
            c.wait_send()

    @pl.when(has_prev)
    def _():
        for t in range(2):
            for part in range(3):
                dc_z(t, part).wait_send()

    @pl.when(has_next)
    def _():
        for t in range(2):
            for part in range(3):
                lat_z(t, part).wait_send()

    for down, there in ((0, has_up), (1, has_down)):

        @pl.when(there)
        def _(down=down):
            dc_row(0, down).wait_send()
            dc_row(1, down).wait_send()
            lat_row(2, down).wait_send()

            @pl.when(has_next)
            def _():
                dc_row(2, down).wait_send()
                dc_row(3, down).wait_send()

            @pl.when(has_prev)
            def _():
                lat_row(0, down).wait_send()


def emit(up, lg, kg, small, up_out, lg_out, kg_out, bias_out, gain_out, shift_out, sem):
    pairs = [(kg.at[i], kg_out.at[i]) for i in range(3)]
    pairs += [(up.at[0, t], up_out.at[0, t]) for t in range(2)]
    pairs += [
        (lg, lg_out),
        (small.at[2:3], bias_out),
        (small.at[1:2], gain_out),
        (small.at[0:1], shift_out),
    ]
    copies = [
        pltpu.make_async_copy(src, dst, sem.at[n]) for n, (src, dst) in enumerate(pairs)
    ]
    for c in copies:
        c.start()
    for c in copies:
        c.wait()


def local(latents, cotangent, gain, bias, kernel, kernel_bias):
    count = 8 * 32 * 160 * (128 // GROUPS)
    hbm = pl.BlockSpec(memory_space=pltpu.HBM)
    vmem = pl.BlockSpec(memory_space=pltpu.VMEM)
    dma = pltpu.SemaphoreType.DMA
    shapes = (
        jax.ShapeDtypeStruct((1, 2, 8, 320, 128), BF16),
        jax.ShapeDtypeStruct((1, 2, 4, 160, 128), BF16),
        jax.ShapeDtypeStruct((3, 3, 384, 128), F32),
    )
    operands = (latents, cotangent, gain[None], bias[None], kernel, kernel_bias[None])
    up, lg, kg, small = pl.pallas_call(
        functools.partial(body, float(count)),
        out_shape=(*shapes, jax.ShapeDtypeStruct((8, 128), F32)),
        in_specs=[hbm] * 6,
        out_specs=(vmem,) * 4,
        scratch_shapes=[
            pltpu.VMEM((8, 128), F32),
            pltpu.VMEM((4, 6, 160, 128), BF16),
            pltpu.VMEM((2, 8, 320, 128), BF16),
            pltpu.VMEM((3, 3, 384, 128), BF16),
            pltpu.VMEM((3, 1152, 128), BF16),
            pltpu.VMEM((4, 6, 160, 128), BF16),
            pltpu.VMEM((6, 8, 160, 384), BF16),
            pltpu.VMEM((4, 6, 160, 384), BF16),
            pltpu.VMEM((176, 128), F32),
            pltpu.VMEM((320, 128), F32),
            pltpu.VMEM((1280, 128), F32),
            pltpu.VMEM((2560, 128), F32),
            pltpu.VMEM((3, 128, 1280), BF16),
            pltpu.VMEM((128, 640), BF16),
            pltpu.VMEM((1280, 128), F32),
            pltpu.VMEM((1280, 128), F32),
            pltpu.VMEM((3, 8, 16, 1152), F32),
            pltpu.VMEM((3, 4, 16, 1152), F32),
            pltpu.VMEM((3, 4, 16, 1152), BF16),
            pltpu.VMEM((3, 4, 16, 1152), BF16),
            pltpu.VMEM((3, 4, 16, 1152), BF16),
            pltpu.VMEM((3, 4, 16, 1152), BF16),
            pltpu.VMEM((3, 8, 16, 1152), BF16),
            pltpu.VMEM((8, 8, 128), F32),
            pltpu.VMEM((4, 8, 128), F32),
            pltpu.VMEM((8, 8, 128), F32),
            pltpu.VMEM((4, 8, 128), F32),
            pltpu.VMEM((4, 8, 128), F32),
            dma((7,)),
            dma((10,)),
            dma((10,)),
            dma((14,)),
            dma((14,)),
            dma((28,)),
            dma((28,)),
            dma((3, 17)),
            dma((3, 17)),
        ],
        compiler_params=pltpu.CompilerParams(
            collective_id=0, has_side_effects=True, vmem_limit_bytes=40 * 1024 * 1024
        ),
        cost_estimate=pl.CostEstimate(flops=3 * 2 * 1280 * 3456 * 128, bytes_accessed=6000000, transcendentals=500000),
    )(*(pltpu.with_memory_space_constraint(a, pltpu.HBM) for a in operands))
    row = jax.ShapeDtypeStruct((1, 128), F32)
    up, lg, kg, bias_grad, gain_grad, shift_grad = pl.pallas_call(
        emit,
        out_shape=(*shapes, row, row, row),
        in_specs=[vmem] * 4,
        out_specs=(hbm,) * 6,
        scratch_shapes=[dma((9,))],
        cost_estimate=pl.CostEstimate(flops=0, bytes_accessed=3500000, transcendentals=0),
    )(*(pltpu.with_memory_space_constraint(a, pltpu.VMEM) for a in (up, lg, kg, small)))
    return up, lg, kg, bias_grad[0], gain_grad[0], shift_grad[0]


def solution(mesh):
    split = P("dp", "tm", "height", None, None)
    return jax.shard_map(
        local,
        mesh=mesh,
        in_specs=(split, split, P(), P(), P(), P()),
        out_specs=(split, split, P(), P(), P(), P()),
        check_vma=False,
    )
```
